256 devices in a mesh: img: 64 (over y, z_lo, x), shell: 4 (over z_hi, core).
Axes of the slice: x: 4, y: 4, z: 8 (z_hi: 2, z_lo: 4; z = z_hi * 4 + z_lo), core: 2. Of those that a mesh axis runs over, the one named last changes fastest.
Arguments:
- images: float32 [1024, 40, 384], P('img', 'shell'), may hold values from -70 to 70
- references: bfloat16 [192, 40, 384], P('img', 'shell'), may hold values from -0.2 to 0.2
- class_offset: int32 [192], replicated, may hold values from 0 to 191
- ctf_group: int32 [1024], P('img'), may hold values from 0 to 15
- ctf: float32 [16, 40], P(None, 'shell'), may hold values from -1 to 1
- noise_power: float32 [40], P('shell'), may hold values from 0.3 to 3
- prior_precision: float32 [40], P('shell'), may hold values from 1 to 10
Outputs:
- new_references: bfloat16 [192, 40, 384], P('img', 'shell')
- log_evidence: float32 [1024], P('img')
The draws below stay inside these ranges and needn't reach their ends.
All inputs are finite; a program needn't handle non-finite values.
Results may differ from the reference program's by a relative error of at most 0.011.
Values may be sent and summed in bfloat16 or wider, within the bound.
No kernel may reach another device: no remote copies, remote signals or barrier semaphores. Data moves between devices by JAX's collectives and lax.ppermute only.
A program may use at most 128 MiB of HBM per device.

```python
import math
import jax
import jax.numpy as jnp
from jax import lax

CYCLES = 40
ANG = 192
ROT = 48
GROUPS = 16
CLASSES = 192
IMAGES = 1024


def shared_references(key):
    sample = jax.random.normal(jax.random.fold_in(key, 11), (CLASSES, CYCLES, 2 * ANG), jnp.float32)
    return 0.03 * jnp.clip(sample, -6.5, 6.5)


def shared_offsets(key):
    seeded = jax.random.fold_in(key, 12)
    values = jax.random.randint(seeded, (CLASSES,), 0, ANG)
    places = jax.random.permutation(jax.random.fold_in(seeded, 1), CLASSES)
    return values.at[places[0]].set(0).at[places[1]].set(ANG - 1).astype(jnp.int32)


def shared_groups(key):
    seeded = jax.random.fold_in(key, 13)
    values = jax.random.randint(seeded, (IMAGES,), 0, GROUPS)
    places = jax.random.permutation(jax.random.fold_in(seeded, 1), IMAGES)
    return values.at[places[0]].set(0).at[places[1]].set(GROUPS - 1).astype(jnp.int32)


def shared_ctf(key):
    return jax.random.uniform(jax.random.fold_in(key, 14), (GROUPS, CYCLES), jnp.float32, -1.0, 1.0)


def shared_noise(key):
    low = math.log(0.3)
    high = math.log(3.0)
    return jnp.exp(jax.random.uniform(jax.random.fold_in(key, 15), (CYCLES,), jnp.float32, low, high))


def draw_images(key, part):
    key = jax.random.fold_in(key, 2)
    return jnp.clip(jax.random.normal(key, (IMAGES, CYCLES, 2 * ANG), jnp.float32), -6.0, 6.0)


def draw_references(key, part):
    values = shared_references(key)
    return values.astype(jnp.bfloat16)


def draw_class_offset(key, part):
    values = shared_offsets(key)
    return values


def draw_ctf_group(key, part):
    values = shared_groups(key)
    return values


def draw_ctf(key, part):
    values = shared_ctf(key)
    return values


def draw_noise_power(key, part):
    values = shared_noise(key)
    return values


def levels(stream_key, shape, split, smallest, top_value):
    def one(dim, shards_of):
        draws = jax.random.uniform(jax.random.fold_in(jax.random.fold_in(stream_key, 6), dim), (shards_of,), jnp.float32, smallest / len(split), top_value / len(split))
        return jnp.repeat(jnp.exp(draws), shape[dim] // shards_of).reshape((-1,) + (1,) * (len(shape) - dim - 1))

    loudness = one(*split[0])
    for cut in split[1:]:
        loudness = loudness * one(*cut)
    return loudness


def setup_inputs(seed: int = 0) -> dict:
    seeds = jax.random.split(jax.random.key(seed), 8)
    images = draw_images(jax.random.fold_in(seeds[7], 71), 0)
    references = draw_references(jax.random.fold_in(seeds[7], 71), 0)
    class_offset = draw_class_offset(jax.random.fold_in(seeds[7], 71), 0)
    ctf_group = draw_ctf_group(jax.random.fold_in(seeds[7], 71), 0)
    ctf = draw_ctf(jax.random.fold_in(seeds[7], 71), 0)
    noise_power = draw_noise_power(jax.random.fold_in(seeds[7], 71), 0)
    prior_precision = jnp.clip(jnp.exp(math.log(10.0) - 2.3025851 * jax.random.uniform(seeds[6], (CYCLES,), jnp.float32) ** levels(seeds[6], (CYCLES,), ((0, 4),), -0.2, 0.2)), 1.0, 10.0)
    return dict(images=images, references=references, class_offset=class_offset, ctf_group=ctf_group, ctf=ctf, noise_power=noise_power, prior_precision=prior_precision)


def reference(images, references, class_offset, ctf_group, ctf, noise_power, prior_precision):
    image_count = images.shape[0]
    coeff_count = CYCLES * 2 * ANG
    angle_step = ANG // ROT
    weight = 1.0 / noise_power
    image_filter = (ctf * weight[None, :])[ctf_group]
    filtered = (images * image_filter[:, :, None]).astype(jnp.bfloat16)
    filtered_wide = filtered.astype(jnp.float32).reshape(image_count, coeff_count)
    cycle_power = jnp.sum(references.astype(jnp.float32) ** 2, axis=2)
    ctf_squared = ctf * ctf * weight[None, :]
    half_norm = 0.5 * jnp.dot(ctf_squared, cycle_power.T, precision=lax.Precision.HIGHEST)
    norm_image = half_norm[:, :][ctf_group]
    angles = jnp.arange(ANG).astype(jnp.int32)
    shifts = (angle_step * jnp.arange(ROT)).astype(jnp.int32)

    def one_class(class_ref, offset):
        indices = ((angles[None, :] - shifts[:, None] - offset) % ANG).astype(jnp.int32)
        source = jnp.broadcast_to(class_ref.reshape(1, 2 * CYCLES, ANG), (ROT, 2 * CYCLES, ANG))
        picks = jnp.broadcast_to(indices[:, None, :], (ROT, 2 * CYCLES, ANG))
        rotated = jnp.take_along_axis(source, picks, axis=2).reshape(ROT, coeff_count)
        return jnp.dot(filtered_wide, rotated.astype(jnp.float32).T, precision=lax.Precision.HIGHEST)

    cross_terms = lax.map(lambda pair: one_class(pair[0], pair[1]), (references, class_offset))
    scores = jnp.transpose(cross_terms, (1, 0, 2)) - norm_image[:, :, None]
    flat_scores = scores.reshape(image_count, CLASSES * ROT)
    largest = jnp.max(flat_scores, axis=1, keepdims=True)
    totals = jnp.sum(jnp.exp(flat_scores - largest), axis=1)
    log_evidence = largest[:, 0] + jnp.log(totals)
    probs = jnp.exp(flat_scores - log_evidence[:, None]).astype(jnp.bfloat16).reshape(image_count, CLASSES, ROT)
    filtered_polar = filtered_wide.reshape(image_count, 2 * CYCLES, ANG)

    def add_rotation(running, inputs):
        rotation, prob_slice = inputs
        indices = ((angles + angle_step * rotation) % ANG).astype(jnp.int32)
        rotated_images = jnp.take(filtered_polar, indices, axis=2).reshape(image_count, coeff_count)
        running = running + jnp.dot(prob_slice.astype(jnp.float32).T, rotated_images, precision=lax.Precision.HIGHEST)
        return running, None

    numerators, _ = lax.scan(add_rotation, jnp.zeros((CLASSES, coeff_count), jnp.float32),
                             (jnp.arange(ROT).astype(jnp.int32), jnp.transpose(probs, (2, 0, 1))))
    back_index = ((angles[None, :] + class_offset[:, None]) % ANG).astype(jnp.int32)
    picks = jnp.broadcast_to(back_index[:, None, :], (CLASSES, 2 * CYCLES, ANG))
    aligned = jnp.take_along_axis(numerators.reshape(CLASSES, 2 * CYCLES, ANG), picks, axis=2)
    class_mass = jnp.sum(probs.astype(jnp.float32), axis=2)
    denominators = jnp.dot(class_mass.T, ctf_squared[ctf_group], precision=lax.Precision.HIGHEST)
    new_references = aligned.reshape(CLASSES, CYCLES, 2 * ANG) / (denominators + prior_precision[None, :])[:, :, None]
    return new_references.astype(jnp.bfloat16), log_evidence
```

```python
import functools

import jax
import jax.numpy as jnp
from jax import lax
from jax.experimental import pallas as pl
from jax.experimental.pallas import tpu as pltpu
from jax.sharding import PartitionSpec as P

ANG = 192
ROT = 48
STEP = ANG // ROT
CYC = 10
ROW = 2 * ANG
TURN = 32
TURNS = ANG // TURN
FINE = TURN // STEP
BLOCK = 2 * CYC * TURN
COEF = TURNS * BLOCK
WIDE = COEF + 128
OWN_IMAGES = 16
OWN_CLASSES = 3
IMG_PEERS = 4
CLS_PEERS = 16
CLS = OWN_CLASSES * CLS_PEERS
ROWS = TURNS * CLS
HALF = FINE * OWN_IMAGES * 2
F32 = jnp.float32
BF16 = jnp.bfloat16
VMEM_LIMIT = 48 * 1024 * 1024


def lanes_of(shape):
    return lax.broadcasted_iota(jnp.int32, shape, len(shape) - 1)


def three_parts(x):
    hi = x.astype(BF16).astype(F32)
    rest = x - hi
    mid = rest.astype(BF16).astype(F32)
    return hi, mid, rest - mid


def pick4(lane, parts):
    return jnp.where(
        lane < 64,
        jnp.where(lane < 32, parts[0], parts[1]),
        jnp.where(lane < 96, parts[2], parts[3]),
    )


def turned_tile(rows_of, w, j, lane):
    parts = []
    for t in range(4):
        p, q = 2 * j + t // 2, t % 2
        start = q * ANG + TURN * w
        vreg, off = start // 128, start % 128
        piece = rows_of[p][:, vreg * 128 : vreg * 128 + 128]
        shift = (32 * t - off) % 128
        parts.append(pltpu.roll(piece, shift, 1) if shift else piece)
    return pick4(lane, parts)


def doubled_roll(x, shift):
    lane = lanes_of(x.shape)
    other = pltpu.roll(x, ANG, 1)
    first = lane < ANG
    a0 = pltpu.roll(jnp.where(first, x, other), shift, 1)
    a1 = pltpu.roll(jnp.where(first, other, x), shift, 1)
    return jnp.where(first, a0, a1)


def prologue_kernel(
    first_ref, offset_ref, group_ref, images_ref, refs_ref, ctf_ref, noise_ref,
    image_msg, class_msg,
    table_f, table_s, filt, square, padded, aligned,
):
    weight = 1.0 / noise_ref[...]
    ctf = ctf_ref[...]
    table_f[...] = jnp.zeros_like(table_f)
    table_s[...] = jnp.zeros_like(table_s)
    table_f[:, :CYC] = ctf * weight
    table_s[:, :CYC] = ctf * ctf * weight
    for i in range(OWN_IMAGES):
        g = group_ref[i]
        filt[i : i + 1, :] = table_f[pl.ds(g, 1), :]
        square[i : i + 1, :] = table_s[pl.ds(g, 1), :]

    lane16 = lanes_of((OWN_IMAGES, 128))
    factors = filt[...]
    rows = []
    for p in range(CYC):
        x = images_ref[:, p, :] * factors[:, p : p + 1]
        rows.append(x.astype(BF16).astype(F32))
    for w in range(TURNS):
        for j in range(5):
            at = w * BLOCK + j * 128
            image_msg[:, at : at + 128] = turned_tile(rows, w, j, lane16).astype(BF16)
    hi, mid, lo = three_parts(square[...])
    extra = hi
    for k, part in enumerate((mid, hi, lo, mid, hi)):
        extra = extra + pltpu.roll(part, 10 * (k + 1), 1)
    image_msg[:, COEF:] = extra.astype(BF16)

    padded[...] = jnp.zeros_like(padded)
    aligned[...] = jnp.zeros_like(aligned)
    for c in range(OWN_CLASSES):
        padded[:CYC, :] = refs_ref[c].astype(F32)
        aligned[c] = doubled_roll(padded[...], offset_ref[first_ref[0] + c])
    lane8 = lanes_of((8, 128))
    rows = [aligned[:, p, :] for p in range(CYC)]
    power = jnp.zeros((8, 128), F32)
    for p in range(CYC):
        power = jnp.where(lane8 == p, jnp.sum(rows[p] * rows[p], axis=1, keepdims=True), power)
    row48 = lax.broadcasted_iota(jnp.int32, (CLS, 128), 0) % OWN_CLASSES

    def spread(tile):
        return jnp.where(
            row48 == 0, tile[0:1], jnp.where(row48 == 1, tile[1:2], tile[2:3])
        ).astype(BF16)

    for w in range(TURNS):
        for j in range(5):
            at = w * BLOCK + j * 128
            class_msg[:, at : at + 128] = spread(turned_tile(rows, w, j, lane8))
    hi, mid, lo = three_parts(-0.5 * power)
    extra = hi
    for k, part in enumerate((hi, mid, hi, mid, lo)):
        extra = extra + pltpu.roll(part, 10 * (k + 1), 1)
    class_msg[:, COEF:] = spread(extra)


def slot_base(place_ref, k):
    owner = place_ref[0] ^ k
    half = (owner >> 1) ^ place_ref[1]
    return half * HALF + (owner & 1) * OWN_IMAGES


def fill_block(image_refs, bases, w, fine_ref):
    lane = lanes_of((OWN_IMAGES, 128))
    inner = lane % TURN
    after = jnp.where(w == TURNS - 1, 0, w + 1)
    for j in range(5):
        here = pl.ds(pl.multiple_of(w * BLOCK + j * 128, 128), 128)
        there = pl.ds(pl.multiple_of(after * BLOCK + j * 128, 128), 128)
        for k in range(IMG_PEERS):
            cur = image_refs[k][:, here]
            fine_ref[pl.ds(pl.multiple_of(bases[k], 16), 16), j * 128 : j * 128 + 128] = cur
            cur = cur.astype(F32)
            nxt = image_refs[k][:, there].astype(F32)
            for rho in range(1, FINE):
                s = STEP * rho
                val = jnp.where(
                    inner < TURN - s, pltpu.roll(cur, 128 - s, 1), pltpu.roll(nxt, TURN - s, 1)
                )
                fine_ref[
                    pl.ds(pl.multiple_of(bases[k] + 32 * rho, 16), 16), j * 128 : j * 128 + 128
                ] = val.astype(BF16)


def fill_extra(image_refs, bases, fine_ref):
    for k in range(IMG_PEERS):
        extra = image_refs[k][:, COEF:]
        for rho in range(FINE):
            fine_ref[pl.ds(pl.multiple_of(bases[k] + 32 * rho, 16), 16), :128] = extra


NT = (((1,), (1,)), ((), ()))


def scores_kernel(place_ref, f0, f1, f2, f3, class_ref, keep_ref, send_ref, fine, stack, total):
    image_refs = (f0, f1, f2, f3)
    bases = [slot_base(place_ref, k) for k in range(IMG_PEERS)]
    fill_extra(image_refs, bases, fine)
    for g in range(TURNS):
        stack[g * CLS : (g + 1) * CLS, :128] = class_ref[:, COEF:]
    total[...] = lax.dot_general(
        stack[:, :128], fine[:, :128], NT, preferred_element_type=F32
    )

    def step(w, carry):
        fill_block(image_refs, bases, w, fine)
        for g in range(TURNS):
            back = jnp.where(w >= g, w - g, w - g + TURNS)
            stack[g * CLS : (g + 1) * CLS, :] = class_ref[
                :, pl.ds(pl.multiple_of(back * BLOCK, 128), BLOCK)
            ]
        total[...] += lax.dot_general(stack[...], fine[...], NT, preferred_element_type=F32)
        return carry

    lax.fori_loop(0, TURNS, step, 0)
    keep_ref[...] = total[:, :HALF]
    send_ref[...] = total[:, HALF:]


def over_rotations(op, x):
    for s in (32, 64, 128):
        x = op(x, pltpu.roll(x, s, 1))
    return x


def stats_kernel(mine_ref, other_ref, scores_ref, stats_ref):
    scores = mine_ref[...] + other_ref[...]
    scores_ref[...] = scores
    big = jnp.max(scores, axis=0, keepdims=True)
    big = over_rotations(jnp.maximum, jnp.broadcast_to(big, (8, HALF)))
    part = jnp.sum(jnp.exp(scores - big[:1]), axis=0, keepdims=True)
    part = over_rotations(jnp.add, jnp.broadcast_to(part, (8, HALF)))
    row = lax.broadcasted_iota(jnp.int32, (8, HALF), 0)
    stats_ref[...] = jnp.where(row < 4, big, part)


def probs_kernel(scores_ref, s0, s1, s2, s3, probs_ref, evidence_ref):
    stats = [s[...] for s in (s0, s1, s2, s3)]
    bigs = [s[0:1] for s in stats]
    parts = [s[4:5] for s in stats]
    largest = jnp.maximum(jnp.maximum(bigs[0], bigs[1]), jnp.maximum(bigs[2], bigs[3]))
    total = sum(p * jnp.exp(b - largest) for b, p in zip(bigs, parts))
    evidence = largest + jnp.log(total)
    probs_ref[...] = jnp.exp(scores_ref[...] - evidence).astype(BF16)
    evidence_ref[...] = jnp.broadcast_to(evidence, (8, HALF))


def sums_kernel(place_ref, f0, f1, f2, f3, keep_ref, other_ref, out_ref, fine, probs, sums):
    image_refs = (f0, f1, f2, f3)
    bases = [slot_base(place_ref, k) for k in range(IMG_PEERS)]
    probs[:, :HALF] = keep_ref[...]
    probs[:, HALF:] = other_ref[...]
    sums[...] = jnp.zeros_like(sums)
    fill_extra(image_refs, bases, fine)
    extra = jnp.dot(probs[...], fine[:, :128], preferred_element_type=F32)
    mass = extra[:CLS]
    for g in range(1, TURNS):
        mass = mass + extra[g * CLS : (g + 1) * CLS]
    mass = mass + pltpu.roll(mass, 118, 1) + pltpu.roll(mass, 98, 1)
    mass = jnp.where(lanes_of((CLS, 128)) < CYC, mass, 0.0)
    hi, mid, lo = three_parts(mass)
    out_ref[:, COEF:] = (hi + pltpu.roll(mid, 10, 1) + pltpu.roll(lo, 20, 1)).astype(BF16)

    def step(w, carry):
        fill_block(image_refs, bases, w, fine)
        turned = jnp.dot(probs[...], fine[...], preferred_element_type=F32)
        for g in range(TURNS):
            back = jnp.where(w >= g, w - g, w - g + TURNS)
            sums[:, pl.ds(pl.multiple_of(back * BLOCK, 128), BLOCK)] += turned[
                g * CLS : (g + 1) * CLS, :
            ]
        return carry

    lax.fori_loop(0, TURNS, step, 0)
    out_ref[:, :COEF] = sums[...].astype(BF16)


def final_kernel(first_ref, offset_ref, msg_ref, prior_ref, out_ref, aligned):
    r = lax.broadcasted_iota(jnp.int32, (16, CLS), 0)
    k = lax.broadcasted_iota(jnp.int32, (16, CLS), 1)
    chosen = jnp.where(k % OWN_CLASSES == r, 1.0, 0.0).astype(BF16)
    total = jnp.dot(chosen, msg_ref[...], preferred_element_type=F32)[:8]
    lane = lanes_of((8, 128))
    extra = total[:, COEF:]
    den = extra + pltpu.roll(extra, 118, 1) + pltpu.roll(extra, 108, 1)
    tiles = {}
    for j in range(5):
        below = []
        for p in (2 * j, 2 * j + 1):
            below.append(den[:, p : p + 1] + prior_ref[0:1, p : p + 1])
        below = jnp.where(lane < 64, below[0], below[1])
        for w in range(TURNS):
            at = w * BLOCK + j * 128
            tiles[w, j] = total[:, at : at + 128] / below
    for p in range(CYC):
        for v in range(3):
            parts = []
            for u in range(4):
                start = 128 * v + 32 * u
                q, w = start // ANG, (start % ANG) // TURN
                t = 2 * (p % 2) + q
                shift = (32 * u - 32 * t) % 128
                piece = tiles[w, p // 2]
                parts.append(pltpu.roll(piece, shift, 1) if shift else piece)
            aligned[:, p, v * 128 : v * 128 + 128] = pick4(lane, parts)
    for c in range(OWN_CLASSES):
        off = offset_ref[first_ref[0] + c]
        back = jnp.where(off == 0, 0, ROW - off)
        out_ref[c] = doubled_roll(aligned[c], back)[:CYC].astype(BF16)


def call(kernel, outs, scratch, specs):
    return pl.pallas_call(
        kernel,
        out_shape=outs,
        in_specs=[pl.BlockSpec(memory_space=s) for s in specs],
        out_specs=jax.tree.map(lambda _: pl.BlockSpec(memory_space=pltpu.VMEM), outs),
        scratch_shapes=scratch,
        compiler_params=pltpu.CompilerParams(vmem_limit_bytes=VMEM_LIMIT),
    )


S, V = pltpu.SMEM, pltpu.VMEM


def shaped(shape, dtype):
    return jax.ShapeDtypeStruct(shape, dtype)


def local(images, references, class_offset, ctf_group, ctf, noise_power, prior_precision):
    img = lax.axis_index("img")
    core = lax.axis_index("shell") % 2
    level = (img // 4) % 4
    first = (img * OWN_CLASSES).astype(jnp.int32).reshape(1)
    place = jnp.stack([level, core]).astype(jnp.int32)

    def along_z(x, k):
        return lax.ppermute(x, "img", [(i, i ^ (4 * k)) for i in range(64)])

    def along_shell(x, k):
        return lax.ppermute(x, "shell", [(i, i ^ k) for i in range(4)])

    groups = [[16 * y + 4 * z + x for y in range(4) for x in range(4)] for z in range(4)]

    def over_classes(x):
        return lax.all_to_all(x, "img", 0, 0, axis_index_groups=groups, tiled=True)

    image_msg, class_msg = call(
        prologue_kernel,
        [shaped((OWN_IMAGES, WIDE), BF16), shaped((CLS, WIDE), BF16)],
        [
            V((16, 128), F32), V((16, 128), F32), V((16, 128), F32), V((16, 128), F32),
            V((16, ROW), F32), V((8, 16, ROW), F32),
        ],
        [S, S, S, V, V, V, V],
    )(first, class_offset, ctf_group, images, references, ctf, noise_power.reshape(1, CYC))
    held = [image_msg] + [along_z(image_msg, k) for k in (1, 2, 3)]
    class_all = over_classes(class_msg)

    keep, send = call(
        scores_kernel,
        [shaped((ROWS, HALF), F32)] * 2,
        [V((2 * HALF, BLOCK), BF16), V((ROWS, BLOCK), BF16), V((ROWS, 2 * HALF), F32)],
        [S, V, V, V, V, V],
    )(place, *held, class_all)
    pair = keep + along_shell(send, 1)
    other = along_shell(pair, 2)
    scores, stats = call(
        stats_kernel, [shaped((ROWS, HALF), F32), shaped((8, HALF), F32)], [], [V, V]
    )(pair, other)
    all_stats = [stats] + [along_z(stats, k) for k in (1, 2, 3)]
    probs, evidence = call(
        probs_kernel, [shaped((ROWS, HALF), BF16), shaped((8, HALF), F32)], [], [V] * 5
    )(scores, *all_stats)
    probs_other = along_shell(probs, 1)
    evidence_other = along_shell(evidence, 1)
    sums = call(
        sums_kernel,
        shaped((CLS, WIDE), BF16),
        [V((2 * HALF, BLOCK), BF16), V((ROWS, 2 * HALF), BF16), V((CLS, COEF), F32)],
        [S] + [V] * 6,
    )(place, *held, probs, probs_other)
    own = over_classes(sums)
    new_references = call(
        final_kernel,
        shaped((OWN_CLASSES, CYC, ROW), BF16),
        [V((8, 16, ROW), F32)],
        [S, S, V, V],
    )(first, class_offset, own, prior_precision.reshape(1, CYC))
    mine = jnp.where(core == level // 2, evidence[0], evidence_other[0])
    log_evidence = lax.dynamic_slice_in_dim(mine, (level % 2) * OWN_IMAGES, OWN_IMAGES)
    return new_references, log_evidence


def solution(mesh):
    placed = (
        P("img", "shell", None),
        P("img", "shell", None),
        P(),
        P("img"),
        P(None, "shell"),
        P("shell"),
        P("shell"),
    )
    return jax.shard_map(
        local,
        mesh=mesh,
        in_specs=placed,
        out_specs=(P("img", "shell", None), P("img")),
        check_vma=False,
    )
```

```python
import functools

import jax
import jax.numpy as jnp
from jax import lax
from jax.experimental import pallas as pl
from jax.experimental.pallas import tpu as pltpu
from jax.sharding import PartitionSpec as P

ANG = 192
ROT = 48
STEP = ANG // ROT
CYC = 10
ROW = 2 * ANG
TURN = 32
TURNS = ANG // TURN
FINE = TURN // STEP
BLOCK = 2 * CYC * TURN
COEF = TURNS * BLOCK
WIDE = COEF + 128
OWN_IMAGES = 16
OWN_CLASSES = 3
IMG_PEERS = 4
CLS_PEERS = 16
CLS = OWN_CLASSES * CLS_PEERS
ROWS = TURNS * CLS
HALF = FINE * OWN_IMAGES * 2
F32 = jnp.float32
BF16 = jnp.bfloat16
VMEM_LIMIT = 24 * 1024 * 1024
VMEM_MOST = 60 * 1024 * 1024


def lanes_of(shape):
    return lax.broadcasted_iota(jnp.int32, shape, len(shape) - 1)


def three_parts(x):
    hi = x.astype(BF16).astype(F32)
    rest = x - hi
    mid = rest.astype(BF16).astype(F32)
    return hi, mid, rest - mid


def pick4(lane, parts):
    return jnp.where(
        lane < 64,
        jnp.where(lane < 32, parts[0], parts[1]),
        jnp.where(lane < 96, parts[2], parts[3]),
    )


def turned_tile(rows_of, w, j, lane):
    parts = []
    for t in range(4):
        p, q = 2 * j + t // 2, t % 2
        start = q * ANG + TURN * w
        vreg, off = start // 128, start % 128
        piece = rows_of[p][:, vreg * 128 : vreg * 128 + 128]
        shift = (32 * t - off) % 128
        parts.append(pltpu.roll(piece, shift, 1) if shift else piece)
    return pick4(lane, parts)


def interleaving(back=False):
    a = lax.broadcasted_iota(jnp.int32, (128, 128), 0)
    b = lax.broadcasted_iota(jnp.int32, (128, 128), 1)
    if back:
        a, b = b, a
    return jnp.where(b == (a % TURN) * 4 + a // TURN, 1.0, 0.0).astype(BF16)


def doubled_roll(x, shift):
    lane = lanes_of(x.shape)
    other = pltpu.roll(x, ANG, 1)
    first = lane < ANG
    a0 = pltpu.roll(jnp.where(first, x, other), shift, 1)
    a1 = pltpu.roll(jnp.where(first, other, x), shift, 1)
    return jnp.where(first, a0, a1)


def turn_classes(stacked, shifts):
    row = lax.broadcasted_iota(jnp.int32, stacked.shape, 0) % 8
    turned = doubled_roll(stacked, shifts[0])
    for c in range(1, OWN_CLASSES):
        turned = jnp.where(row == c, doubled_roll(stacked, shifts[c]), turned)
    return turned


def prologue_kernel(
    first_ref, offset_ref, group_ref, images_ref, refs_ref, ctf_ref, noise_ref,
    image_msg, class_msg,
    table_f, table_s, filt, square, stacked, own,
):
    stacked[...] = jnp.zeros_like(stacked)
    for p in range(CYC):
        stacked[p * 8 : p * 8 + OWN_CLASSES, :] = refs_ref[p].astype(F32)
    turned = turn_classes(
        stacked[...], [offset_ref[first_ref[0] + c] for c in range(OWN_CLASSES)]
    )
    rows = [turned[p * 8 : p * 8 + 8] for p in range(CYC)]
    lane8 = lanes_of((8, 128))
    power = jnp.zeros((8, 128), F32)
    for p in range(CYC):
        power = jnp.where(lane8 == p, jnp.sum(rows[p] * rows[p], axis=1, keepdims=True), power)
    mixing = interleaving()
    for w in range(TURNS):
        tiles = [turned_tile(rows, w, j, lane8) for j in range(5)]
        tiles = jnp.concatenate(tiles, axis=0).astype(BF16)
        tiles = jnp.dot(tiles, mixing, preferred_element_type=F32)
        for j in range(5):
            at = w * BLOCK + j * 128
            own[:, at : at + 128] = tiles[j * 8 : j * 8 + 8]
    hi, mid, lo = three_parts(-0.5 * power)
    extra = hi
    for k, part in enumerate((hi, mid, hi, mid, lo)):
        extra = extra + pltpu.roll(part, 10 * (k + 1), 1)
    own[:, COEF:] = extra
    held = own[:OWN_CLASSES, :].astype(BF16)
    for d in range(CLS_PEERS):
        class_msg[d] = held

    weight = 1.0 / noise_ref[...]
    ctf = ctf_ref[...]
    table_f[...] = jnp.zeros_like(table_f)
    table_s[...] = jnp.zeros_like(table_s)
    table_f[:, :CYC] = ctf * weight
    table_s[:, :CYC] = ctf * ctf * weight
    for i in range(OWN_IMAGES):
        g = group_ref[i]
        filt[i : i + 1, :] = table_f[pl.ds(g, 1), :]
        square[i : i + 1, :] = table_s[pl.ds(g, 1), :]
    lane16 = lanes_of((OWN_IMAGES, 128))
    factors = filt[...]
    rows = []
    for p in range(CYC):
        x = images_ref[p] * factors[:, p : p + 1]
        rows.append(x.astype(BF16).astype(F32))
    for w in range(TURNS):
        tiles = [turned_tile(rows, w, j, lane16) for j in range(5)]
        tiles = jnp.concatenate(tiles, axis=0).astype(BF16)
        tiles = jnp.dot(tiles, mixing, preferred_element_type=F32).astype(BF16)
        for j in range(5):
            at = w * BLOCK + j * 128
            image_msg[:, at : at + 128] = tiles[j * 16 : j * 16 + 16]
    hi, mid, lo = three_parts(square[...])
    extra = hi
    for k, part in enumerate((mid, hi, lo, mid, hi)):
        extra = extra + pltpu.roll(part, 10 * (k + 1), 1)
    image_msg[:, COEF:] = extra.astype(BF16)


QUARTER = HALF // 2


def turned_on(cur, nxt, steps):
    s = 4 * STEP * steps
    lane = lanes_of(cur.shape)
    return pltpu.roll(jnp.where(lane >= s, cur, nxt), 128 - s, 1)


def early_kernel(place_ref, f0, f1, f2, f3, early_ref):
    image_refs = (f0, f1, f2, f3)
    bases = []
    for k in range(IMG_PEERS):
        owner = place_ref[0] ^ k
        half = (owner >> 1) ^ place_ref[1]
        bases.append(half * QUARTER + (owner & 1) * OWN_IMAGES)
    for k in range(IMG_PEERS):
        extra = image_refs[k][:, COEF:]
        for rho in range(FINE // 2):
            early_ref[pl.ds(pl.multiple_of(bases[k] + 32 * rho, 16), 16), COEF:] = extra

    def step(w, carry):
        after = jnp.where(w == TURNS - 1, 0, w + 1)
        for j in range(5):
            here = pl.ds(pl.multiple_of(w * BLOCK + j * 128, 128), 128)
            there = pl.ds(pl.multiple_of(after * BLOCK + j * 128, 128), 128)
            for k in range(IMG_PEERS):
                cur = image_refs[k][:, here]
                nxt = image_refs[k][:, there]
                for rho in range(FINE // 2):
                    val = turned_on(cur, nxt, rho) if rho else cur
                    early_ref[pl.ds(pl.multiple_of(bases[k] + 32 * rho, 16), 16), here] = val
        return carry

    lax.fori_loop(0, TURNS, step, 0)


def make_late(early_ref, late_ref):
    late_ref[:, COEF:] = early_ref[:, COEF:]

    def step(w, carry):
        after = jnp.where(w == TURNS - 1, 0, w + 1)
        for j in range(5):
            here = pl.ds(pl.multiple_of(w * BLOCK + j * 128, 128), 128)
            there = pl.ds(pl.multiple_of(after * BLOCK + j * 128, 128), 128)
            late_ref[:, here] = turned_on(early_ref[:, here], early_ref[:, there], FINE // 2)
        return carry

    lax.fori_loop(0, TURNS, step, 0)


NT = (((1,), (1,)), ((), ()))


def scores_kernel(early_ref, class_ref, keep_ref, send_ref, stack, late):
    for g in range(TURNS):
        rows = slice(g * CLS, (g + 1) * CLS)
        cut = COEF - g * BLOCK
        stack[rows, g * BLOCK : COEF] = class_ref[:, :cut]
        if g:
            stack[rows, : g * BLOCK] = class_ref[:, cut:COEF]
        stack[rows, COEF:] = class_ref[:, COEF:]
    part = lax.dot_general(stack[...], early_ref[...], NT, preferred_element_type=F32)
    keep_ref[:, :QUARTER] = part[:, :QUARTER]
    send_ref[:, :QUARTER] = part[:, QUARTER:]
    make_late(early_ref, late)
    part = lax.dot_general(stack[...], late[...], NT, preferred_element_type=F32)
    keep_ref[:, QUARTER:] = part[:, :QUARTER]
    send_ref[:, QUARTER:] = part[:, QUARTER:]


def over_rotations(op, x):
    for s in (32, 64, 128):
        x = op(x, pltpu.roll(x, s, 1))
    return x


def stats_kernel(mine_ref, other_ref, scores_ref, stats_ref):
    scores = mine_ref[...] + other_ref[...]
    scores_ref[...] = scores
    big = jnp.max(scores, axis=0, keepdims=True)
    big = over_rotations(jnp.maximum, jnp.broadcast_to(big, (8, HALF)))
    part = jnp.sum(jnp.exp(scores - big[:1]), axis=0, keepdims=True)
    part = over_rotations(jnp.add, jnp.broadcast_to(part, (8, HALF)))
    row = lax.broadcasted_iota(jnp.int32, (8, HALF), 0)
    stats_ref[...] = jnp.where(row < 4, big, part)


def probs_kernel(scores_ref, s0, s1, s2, s3, probs_ref, evidence_ref):
    stats = [s[...] for s in (s0, s1, s2, s3)]
    bigs = [s[0:1] for s in stats]
    parts = [s[4:5] for s in stats]
    largest = jnp.maximum(jnp.maximum(bigs[0], bigs[1]), jnp.maximum(bigs[2], bigs[3]))
    total = sum(p * jnp.exp(b - largest) for b, p in zip(bigs, parts))
    evidence = largest + jnp.log(total)
    probs_ref[...] = jnp.exp(scores_ref[...] - evidence).astype(BF16)
    evidence_ref[...] = jnp.broadcast_to(evidence, (8, HALF))


def sums_kernel(early_ref, late_ref, keep_ref, other_ref, out_ref, probs, sums):
    probs[:, :QUARTER] = keep_ref[:, :QUARTER]
    probs[:, QUARTER:HALF] = other_ref[:, :QUARTER]
    probs[:, HALF : HALF + QUARTER] = keep_ref[:, QUARTER:]
    probs[:, HALF + QUARTER :] = other_ref[:, QUARTER:]
    for w in range(0, TURNS, 2):
        span = slice(w * BLOCK, (w + 2) * BLOCK + (128 if w == TURNS - 2 else 0))
        turned = jnp.dot(
            probs[:, :HALF], early_ref[:, span], preferred_element_type=F32
        ) + jnp.dot(probs[:, HALF:], late_ref[:, span], preferred_element_type=F32)
        for b in (w, w + 1):
            for g in range(TURNS):
                back = (b - g) % TURNS
                at = slice(back * BLOCK, (back + 1) * BLOCK)
                term = turned[g * CLS : (g + 1) * CLS, (b - w) * BLOCK : (b - w + 1) * BLOCK]
                if b == 0:
                    sums[:, at] = term
                else:
                    sums[:, at] += term
        if w == TURNS - 2:
            mass = turned[:CLS, 2 * BLOCK :]
            for g in range(1, TURNS):
                mass = mass + turned[g * CLS : (g + 1) * CLS, 2 * BLOCK :]
    mass = mass + pltpu.roll(mass, 118, 1) + pltpu.roll(mass, 98, 1)
    mass = jnp.where(lanes_of((CLS, 128)) < CYC, mass, 0.0)
    hi, mid, lo = three_parts(mass)
    sums[:, COEF:] = hi + pltpu.roll(mid, 10, 1) + pltpu.roll(lo, 20, 1)
    for d in range(CLS_PEERS):
        out_ref[d] = sums[d * OWN_CLASSES : (d + 1) * OWN_CLASSES, :].astype(BF16)


def final_kernel(first_ref, offset_ref, msg_ref, prior_ref, out_ref):
    r = lax.broadcasted_iota(jnp.int32, (16, CLS), 0)
    k = lax.broadcasted_iota(jnp.int32, (16, CLS), 1)
    chosen = jnp.where(k % OWN_CLASSES == r, 1.0, 0.0).astype(BF16)
    total = jnp.dot(chosen, msg_ref[...], preferred_element_type=F32)[:8]
    lane = lanes_of((8, 128))
    extra = total[:, COEF:]
    den = extra + pltpu.roll(extra, 118, 1) + pltpu.roll(extra, 108, 1)
    tiles = {}
    for j in range(5):
        below = []
        for p in (2 * j, 2 * j + 1):
            below.append(den[:, p : p + 1] + prior_ref[0:1, p : p + 1])
        below = jnp.where(lane % 4 < 2, below[0], below[1])
        for w in range(TURNS):
            at = w * BLOCK + j * 128
            tiles[w, j] = total[:, at : at + 128] / below
    keys = list(tiles)
    flat = jnp.concatenate([tiles[k] for k in keys], axis=0).astype(BF16)
    flat = jnp.dot(flat, interleaving(back=True), preferred_element_type=F32)
    tiles = {k: flat[8 * n : 8 * n + 8] for n, k in enumerate(keys)}
    rows = []
    for p in range(CYC):
        vregs = []
        for v in range(3):
            parts = []
            for u in range(4):
                start = 128 * v + 32 * u
                q, w = start // ANG, (start % ANG) // TURN
                t = 2 * (p % 2) + q
                shift = (32 * u - 32 * t) % 128
                piece = tiles[w, p // 2]
                parts.append(pltpu.roll(piece, shift, 1) if shift else piece)
            vregs.append(pick4(lane, parts))
        rows.append(jnp.concatenate(vregs, axis=1))
    shifts = []
    for c in range(OWN_CLASSES):
        off = offset_ref[first_ref[0] + c]
        shifts.append(jnp.where(off == 0, 0, ROW - off))
    turned = turn_classes(jnp.concatenate(rows, axis=0), shifts)
    for p in range(CYC):
        out_ref[p] = turned[p * 8 : p * 8 + OWN_CLASSES].astype(BF16)


def call(kernel, outs, scratch, specs, limit=VMEM_LIMIT, cost=None):
    return pl.pallas_call(
        kernel,
        out_shape=outs,
        in_specs=[pl.BlockSpec(memory_space=s) for s in specs],
        out_specs=jax.tree.map(lambda _: pl.BlockSpec(memory_space=pltpu.VMEM), outs),
        scratch_shapes=scratch,
        compiler_params=pltpu.CompilerParams(vmem_limit_bytes=limit),
        cost_estimate=cost,
    )


S, V = pltpu.SMEM, pltpu.VMEM


def shaped(shape, dtype):
    return jax.ShapeDtypeStruct(shape, dtype)


def local(images, references, class_offset, ctf_group, ctf, noise_power, prior_precision):
    img = lax.axis_index("img")
    core = lax.axis_index("shell") % 2
    level = (img // 4) % 4
    first = (img * OWN_CLASSES).astype(jnp.int32).reshape(1)
    place = jnp.stack([level, core]).astype(jnp.int32)

    def along_peers(x, k):
        return lax.ppermute(x, "img", [(i, i ^ (4 * k)) for i in range(64)])

    def along_shell(x, k):
        return lax.ppermute(x, "shell", [(i, i ^ k) for i in range(4)])

    groups = [[16 * y + 4 * z + x for y in range(4) for x in range(4)] for z in range(4)]

    def over_classes(x):
        return lax.all_to_all(x, "img", 0, 0, axis_index_groups=groups, tiled=True)

    image_msg, class_msg = call(
        prologue_kernel,
        [shaped((OWN_IMAGES, WIDE), BF16), shaped((CLS_PEERS, OWN_CLASSES, WIDE), BF16)],
        [V((16, 128), F32)] * 4 + [V((CYC * 8, ROW), F32), V((8, WIDE), F32)],
        [S, S, S, V, V, V, V],
        VMEM_MOST,
    )(
        first, class_offset, ctf_group, jnp.transpose(images, (1, 0, 2)),
        jnp.transpose(references, (1, 0, 2)), ctf, noise_power.reshape(1, CYC),
    )
    held = [image_msg] + [along_peers(image_msg, k) for k in (1, 2, 3)]
    class_all = over_classes(class_msg).reshape(CLS, WIDE)
    early = call(
        early_kernel,
        shaped((HALF, WIDE), BF16),
        [],
        [S] + [V] * 4,
        cost=pl.CostEstimate(flops=10**13, transcendentals=0, bytes_accessed=10**10),
    )(place, *held)
    keep, send = call(
        scores_kernel,
        [shaped((ROWS, HALF), F32)] * 2,
        [V((ROWS, WIDE), BF16), V((HALF, WIDE), BF16)],
        [V, V],
    )(early, class_all)
    pair = keep + along_shell(send, 1)
    other = along_shell(pair, 2)
    early, pair = lax.optimization_barrier((early, pair))
    late = call(make_late, shaped((HALF, WIDE), BF16), [], [V])(early)
    late, other = lax.optimization_barrier((late, other))
    scores, stats = call(
        stats_kernel, [shaped((ROWS, HALF), F32), shaped((8, HALF), F32)], [], [V, V]
    )(pair, other)
    all_stats = [stats] + [along_peers(stats, k) for k in (1, 2, 3)]
    probs, evidence = call(
        probs_kernel, [shaped((ROWS, HALF), BF16), shaped((8, HALF), F32)], [], [V] * 5
    )(scores, *all_stats)
    probs_other = along_shell(probs, 1)
    evidence_other = along_shell(evidence, 1)
    sums = call(
        sums_kernel,
        shaped((CLS_PEERS, OWN_CLASSES, WIDE), BF16),
        [V((ROWS, 2 * HALF), BF16), V((CLS, WIDE), F32)],
        [V] * 4,
    )(early, late, probs, probs_other)
    own = over_classes(sums).reshape(CLS, WIDE)
    new_references = call(
        final_kernel,
        shaped((CYC, OWN_CLASSES, ROW), BF16),
        [],
        [S, S, V, V],
    )(first, class_offset, own, prior_precision.reshape(1, CYC))
    mine = jnp.where(core == level // 2, evidence[0], evidence_other[0])
    log_evidence = lax.dynamic_slice_in_dim(mine, (level % 2) * OWN_IMAGES, OWN_IMAGES)
    return jnp.transpose(new_references, (1, 0, 2)), log_evidence


def solution(mesh):
    placed = (
        P("img", "shell", None),
        P("img", "shell", None),
        P(),
        P("img"),
        P(None, "shell"),
        P("shell"),
        P("shell"),
    )
    return jax.shard_map(
        local,
        mesh=mesh,
        in_specs=placed,
        out_specs=(P("img", "shell", None), P("img")),
        check_vma=False,
    )
```

```python
import functools

import jax
import jax.numpy as jnp
from jax import lax
from jax.experimental import pallas as pl
from jax.experimental.pallas import tpu as pltpu
from jax.sharding import PartitionSpec as P

ANG = 192
ROT = 48
STEP = ANG // ROT
CYC = 10
ROW = 2 * ANG
TURN = 32
TURNS = ANG // TURN
FINE = TURN // STEP
BLOCK = 2 * CYC * TURN
COEF = TURNS * BLOCK
WIDE = COEF + 128
OWN_IMAGES = 16
OWN_CLASSES = 3
IMG_PEERS = 4
CLS_PEERS = 16
CLS = OWN_CLASSES * CLS_PEERS
TILES = WIDE // 128
SLOT = 32
CHUNK = OWN_CLASSES * SLOT
ROWS = TURNS * CLS
HALF = FINE * OWN_IMAGES * 2
F32 = jnp.float32
BF16 = jnp.bfloat16
VMEM_LIMIT = 24 * 1024 * 1024
VMEM_MOST = 60 * 1024 * 1024


def lanes_of(shape):
    return lax.broadcasted_iota(jnp.int32, shape, len(shape) - 1)


def three_parts(x):
    hi = x.astype(BF16).astype(F32)
    rest = x - hi
    mid = rest.astype(BF16).astype(F32)
    return hi, mid, rest - mid


def pick4(lane, parts):
    return jnp.where(
        lane < 64,
        jnp.where(lane < 32, parts[0], parts[1]),
        jnp.where(lane < 96, parts[2], parts[3]),
    )


def turned_tile(rows_of, w, j, lane):
    parts = []
    for t in range(4):
        p, q = 2 * j + t // 2, t % 2
        start = q * ANG + TURN * w
        vreg, off = start // 128, start % 128
        piece = rows_of[p][:, vreg * 128 : vreg * 128 + 128]
        shift = (32 * t - off) % 128
        parts.append(pltpu.roll(piece, shift, 1) if shift else piece)
    return pick4(lane, parts)


def interleaving(back=False):
    a = lax.broadcasted_iota(jnp.int32, (128, 128), 0)
    b = lax.broadcasted_iota(jnp.int32, (128, 128), 1)
    if back:
        a, b = b, a
    return jnp.where(b == (a % TURN) * 4 + a // TURN, 1.0, 0.0).astype(BF16)


def doubled_roll(x, shift):
    lane = lanes_of(x.shape)
    other = pltpu.roll(x, ANG, 1)
    first = lane < ANG
    a0 = pltpu.roll(jnp.where(first, x, other), shift, 1)
    a1 = pltpu.roll(jnp.where(first, other, x), shift, 1)
    return jnp.where(first, a0, a1)


def turn_classes(stacked, shifts):
    row = lax.broadcasted_iota(jnp.int32, stacked.shape, 0) % 8
    turned = doubled_roll(stacked, shifts[0])
    for c in range(1, OWN_CLASSES):
        turned = jnp.where(row == c, doubled_roll(stacked, shifts[c]), turned)
    return turned


def prologue_kernel(
    first_ref, offset_ref, group_ref, images_ref, refs_ref, ctf_ref, noise_ref,
    image_msg, class_msg,
    table_f, table_s, filt, square, stacked, own,
):
    stacked[...] = jnp.zeros_like(stacked)
    for p in range(CYC):
        stacked[p * 8 : p * 8 + OWN_CLASSES, :] = refs_ref[p].astype(F32)
    turned = turn_classes(
        stacked[...], [offset_ref[first_ref[0] + c] for c in range(OWN_CLASSES)]
    )
    rows = [turned[p * 8 : p * 8 + 8] for p in range(CYC)]
    lane8 = lanes_of((8, 128))
    power = jnp.zeros((8, 128), F32)
    for p in range(CYC):
        power = jnp.where(lane8 == p, jnp.sum(rows[p] * rows[p], axis=1, keepdims=True), power)
    mixing = interleaving()
    own[...] = jnp.zeros_like(own)
    for w in range(TURNS):
        tiles = [turned_tile(rows, w, j, lane8) for j in range(5)]
        tiles = jnp.concatenate(tiles, axis=0).astype(BF16)
        tiles = jnp.dot(tiles, mixing, preferred_element_type=F32)
        for j in range(5):
            own[pl.ds(w * 5 + j, OWN_CLASSES, stride=SLOT), :] = tiles[
                j * 8 : j * 8 + OWN_CLASSES
            ]
    hi, mid, lo = three_parts(-0.5 * power)
    extra = hi
    for k, part in enumerate((hi, mid, hi, mid, lo)):
        extra = extra + pltpu.roll(part, 10 * (k + 1), 1)
    own[pl.ds(TILES - 1, OWN_CLASSES, stride=SLOT), :] = extra[:OWN_CLASSES]
    held = own[...].astype(BF16)
    for d in range(CLS_PEERS):
        class_msg[d * CHUNK : (d + 1) * CHUNK, :] = held

    weight = 1.0 / noise_ref[...]
    ctf = ctf_ref[...]
    table_f[...] = jnp.zeros_like(table_f)
    table_s[...] = jnp.zeros_like(table_s)
    table_f[:, :CYC] = ctf * weight
    table_s[:, :CYC] = ctf * ctf * weight
    for i in range(OWN_IMAGES):
        g = group_ref[i]
        filt[i : i + 1, :] = table_f[pl.ds(g, 1), :]
        square[i : i + 1, :] = table_s[pl.ds(g, 1), :]
    lane16 = lanes_of((OWN_IMAGES, 128))
    factors = filt[...]
    rows = []
    for p in range(CYC):
        x = images_ref[p] * factors[:, p : p + 1]
        rows.append(x.astype(BF16).astype(F32))
    for w in range(TURNS):
        tiles = [turned_tile(rows, w, j, lane16) for j in range(5)]
        tiles = jnp.concatenate(tiles, axis=0).astype(BF16)
        tiles = jnp.dot(tiles, mixing, preferred_element_type=F32).astype(BF16)
        for j in range(5):
            at = w * BLOCK + j * 128
            image_msg[:, at : at + 128] = tiles[j * 16 : j * 16 + 16]
    hi, mid, lo = three_parts(square[...])
    extra = hi
    for k, part in enumerate((mid, hi, lo, mid, hi)):
        extra = extra + pltpu.roll(part, 10 * (k + 1), 1)
    image_msg[:, COEF:] = extra.astype(BF16)


QUARTER = HALF // 2


def turned_on(cur, nxt, steps):
    s = 4 * STEP * steps
    lane = lanes_of(cur.shape)
    return pltpu.roll(jnp.where(lane >= s, cur, nxt), 128 - s, 1)


def tile_pairs():
    for w in range(TURNS):
        for j in range(5):
            here = w * BLOCK + j * 128
            there = (w + 1) % TURNS * BLOCK + j * 128
            yield slice(here, here + 128), slice(there, there + 128)


def early_kernel(place_ref, f0, f1, f2, f3, early_ref):
    image_refs = (f0, f1, f2, f3)
    bases = []
    for k in range(IMG_PEERS):
        owner = place_ref[0] ^ k
        half = (owner >> 1) ^ place_ref[1]
        bases.append(half * QUARTER + (owner & 1) * OWN_IMAGES)
    for k in range(IMG_PEERS):
        extra = image_refs[k][:, COEF:]
        for rho in range(FINE // 2):
            early_ref[pl.ds(pl.multiple_of(bases[k] + 32 * rho, 16), 16), COEF:] = extra

    for here, there in tile_pairs():
        for k in range(IMG_PEERS):
            cur = image_refs[k][:, here]
            nxt = image_refs[k][:, there]
            for rho in range(FINE // 2):
                val = turned_on(cur, nxt, rho) if rho else cur
                early_ref[pl.ds(pl.multiple_of(bases[k] + 32 * rho, 16), 16), here] = val


def make_late(early_ref, late_ref):
    late_ref[:, COEF:] = early_ref[:, COEF:]
    for here, there in tile_pairs():
        late_ref[:, here] = turned_on(early_ref[:, here], early_ref[:, there], FINE // 2)


NT = (((1,), (1,)), ((), ()))


def scores_kernel(early_ref, class_ref, keep_ref, send_ref, wide, stack, late):
    wide[...] = class_ref[...].astype(F32)
    for v in range(TILES):
        for c in range(OWN_CLASSES):
            tile = wide[pl.ds(c * SLOT + v, CLS_PEERS, stride=CHUNK), :].astype(BF16)
            for g in range(TURNS):
                row = g * CLS + c * CLS_PEERS
                at = v * 128 if v == TILES - 1 else (v * 128 + g * BLOCK) % COEF
                stack[row : row + CLS_PEERS, at : at + 128] = tile
    part = lax.dot_general(stack[...], early_ref[...], NT, preferred_element_type=F32)
    keep_ref[:, :QUARTER] = part[:, :QUARTER]
    send_ref[:, :QUARTER] = part[:, QUARTER:]
    make_late(early_ref, late)
    part = lax.dot_general(stack[...], late[...], NT, preferred_element_type=F32)
    keep_ref[:, QUARTER:] = part[:, :QUARTER]
    send_ref[:, QUARTER:] = part[:, QUARTER:]


def over_rotations(op, x):
    for s in (32, 64, 128):
        x = op(x, pltpu.roll(x, s, 1))
    return x


def stats_kernel(mine_ref, other_ref, scores_ref, stats_ref):
    scores = mine_ref[...] + other_ref[...]
    scores_ref[...] = scores
    big = jnp.max(scores, axis=0, keepdims=True)
    big = over_rotations(jnp.maximum, jnp.broadcast_to(big, (8, HALF)))
    part = jnp.sum(jnp.exp(scores - big[:1]), axis=0, keepdims=True)
    part = over_rotations(jnp.add, jnp.broadcast_to(part, (8, HALF)))
    row = lax.broadcasted_iota(jnp.int32, (8, HALF), 0)
    stats_ref[...] = jnp.where(row < 4, big, part)


def probs_kernel(scores_ref, s0, s1, s2, s3, probs_ref, evidence_ref):
    stats = [s[...] for s in (s0, s1, s2, s3)]
    bigs = [s[0:1] for s in stats]
    parts = [s[4:5] for s in stats]
    largest = jnp.maximum(jnp.maximum(bigs[0], bigs[1]), jnp.maximum(bigs[2], bigs[3]))
    total = sum(p * jnp.exp(b - largest) for b, p in zip(bigs, parts))
    evidence = largest + jnp.log(total)
    probs_ref[...] = jnp.exp(scores_ref[...] - evidence).astype(BF16)
    evidence_ref[...] = jnp.broadcast_to(evidence, (8, HALF))


def sums_kernel(early_ref, late_ref, keep_ref, other_ref, out_ref, probs, sums, packed):
    probs[:, :QUARTER] = keep_ref[:, :QUARTER]
    probs[:, QUARTER:HALF] = other_ref[:, :QUARTER]
    probs[:, HALF : HALF + QUARTER] = keep_ref[:, QUARTER:]
    probs[:, HALF + QUARTER :] = other_ref[:, QUARTER:]
    for w in range(0, TURNS, 2):
        span = slice(w * BLOCK, (w + 2) * BLOCK + (128 if w == TURNS - 2 else 0))
        turned = jnp.dot(
            probs[:, :HALF], early_ref[:, span], preferred_element_type=F32
        ) + jnp.dot(probs[:, HALF:], late_ref[:, span], preferred_element_type=F32)
        for b in (w, w + 1):
            for g in range(TURNS):
                back = (b - g) % TURNS
                at = slice(back * BLOCK, (back + 1) * BLOCK)
                term = turned[g * CLS : (g + 1) * CLS, (b - w) * BLOCK : (b - w + 1) * BLOCK]
                if b == 0:
                    sums[:, at] = term
                else:
                    sums[:, at] += term
        if w == TURNS - 2:
            mass = turned[:CLS, 2 * BLOCK :]
            for g in range(1, TURNS):
                mass = mass + turned[g * CLS : (g + 1) * CLS, 2 * BLOCK :]
    mass = mass + pltpu.roll(mass, 118, 1) + pltpu.roll(mass, 98, 1)
    mass = jnp.where(lanes_of((CLS, 128)) < CYC, mass, 0.0)
    hi, mid, lo = three_parts(mass)
    sums[:, COEF:] = hi + pltpu.roll(mid, 10, 1) + pltpu.roll(lo, 20, 1)
    for c in range(OWN_CLASSES):
        rows = slice(c * CLS_PEERS, (c + 1) * CLS_PEERS)
        for v in range(SLOT):
            tile = sums[rows, v * 128 : v * 128 + 128] if v < TILES else jnp.zeros((16, 128), F32)
            packed[pl.ds(c * SLOT + v, CLS_PEERS, stride=CHUNK), :] = tile
    out_ref[...] = packed[...].astype(BF16)


def final_kernel(first_ref, offset_ref, msg_ref, prior_ref, out_ref, summed):
    total = msg_ref[:CHUNK, :].astype(F32)
    for d in range(1, CLS_PEERS):
        total = total + msg_ref[d * CHUNK : (d + 1) * CHUNK, :].astype(F32)
    summed[:CHUNK, :] = total
    summed[CHUNK:, :] = jnp.zeros((8 * SLOT - CHUNK, 128), F32)
    lane = lanes_of((8, 128))
    extra = summed[pl.ds(TILES - 1, 8, stride=SLOT), :]
    den = extra + pltpu.roll(extra, 118, 1) + pltpu.roll(extra, 108, 1)
    tiles = {}
    for j in range(5):
        below = []
        for p in (2 * j, 2 * j + 1):
            below.append(den[:, p : p + 1] + prior_ref[0:1, p : p + 1])
        below = jnp.where(lane % 4 < 2, below[0], below[1])
        for w in range(TURNS):
            tiles[w, j] = summed[pl.ds(w * 5 + j, 8, stride=SLOT), :] / below
    keys = list(tiles)
    flat = jnp.concatenate([tiles[k] for k in keys], axis=0).astype(BF16)
    flat = jnp.dot(flat, interleaving(back=True), preferred_element_type=F32)
    tiles = {k: flat[8 * n : 8 * n + 8] for n, k in enumerate(keys)}
    rows = []
    for p in range(CYC):
        vregs = []
        for v in range(3):
            parts = []
            for u in range(4):
                start = 128 * v + 32 * u
                q, w = start // ANG, (start % ANG) // TURN
                t = 2 * (p % 2) + q
                shift = (32 * u - 32 * t) % 128
                piece = tiles[w, p // 2]
                parts.append(pltpu.roll(piece, shift, 1) if shift else piece)
            vregs.append(pick4(lane, parts))
        rows.append(jnp.concatenate(vregs, axis=1))
    shifts = []
    for c in range(OWN_CLASSES):
        off = offset_ref[first_ref[0] + c]
        shifts.append(jnp.where(off == 0, 0, ROW - off))
    turned = turn_classes(jnp.concatenate(rows, axis=0), shifts)
    for p in range(CYC):
        out_ref[p] = turned[p * 8 : p * 8 + OWN_CLASSES].astype(BF16)


def call(kernel, outs, scratch, specs, limit=VMEM_LIMIT, cost=None):
    return pl.pallas_call(
        kernel,
        out_shape=outs,
        in_specs=[pl.BlockSpec(memory_space=s) for s in specs],
        out_specs=jax.tree.map(lambda _: pl.BlockSpec(memory_space=pltpu.VMEM), outs),
        scratch_shapes=scratch,
        compiler_params=pltpu.CompilerParams(vmem_limit_bytes=limit),
        cost_estimate=cost,
    )


S, V = pltpu.SMEM, pltpu.VMEM


def shaped(shape, dtype):
    return jax.ShapeDtypeStruct(shape, dtype)


def local(images, references, class_offset, ctf_group, ctf, noise_power, prior_precision):
    img = lax.axis_index("img")
    core = lax.axis_index("shell") % 2
    level = (img // 4) % 4
    first = (img * OWN_CLASSES).astype(jnp.int32).reshape(1)
    place = jnp.stack([level, core]).astype(jnp.int32)

    def along_peers(x, k):
        return lax.ppermute(x, "img", [(i, i ^ (4 * k)) for i in range(64)])

    def along_shell(x, k):
        return lax.ppermute(x, "shell", [(i, i ^ k) for i in range(4)])

    groups = [[16 * y + 4 * z + x for y in range(4) for x in range(4)] for z in range(4)]

    def over_classes(x):
        return lax.all_to_all(x, "img", 0, 0, axis_index_groups=groups, tiled=True)

    image_msg, class_msg = call(
        prologue_kernel,
        [shaped((OWN_IMAGES, WIDE), BF16), shaped((CLS_PEERS * CHUNK, 128), BF16)],
        [V((16, 128), F32)] * 4 + [V((CYC * 8, ROW), F32), V((CHUNK, 128), F32)],
        [S, S, S, V, V, V, V],
        VMEM_MOST,
    )(
        first, class_offset, ctf_group, jnp.transpose(images, (1, 0, 2)),
        jnp.transpose(references, (1, 0, 2)), ctf, noise_power.reshape(1, CYC),
    )
    held = [image_msg] + [along_peers(image_msg, k) for k in (1, 2, 3)]
    class_all = over_classes(class_msg)
    early = call(
        early_kernel,
        shaped((HALF, WIDE), BF16),
        [],
        [S] + [V] * 4,
        cost=pl.CostEstimate(flops=10**13, transcendentals=0, bytes_accessed=10**10),
    )(place, *held)
    keep, send = call(
        scores_kernel,
        [shaped((ROWS, HALF), F32)] * 2,
        [V((CLS_PEERS * CHUNK, 128), F32), V((ROWS, WIDE), BF16), V((HALF, WIDE), BF16)],
        [V, V],
    )(early, class_all)
    pair = keep + along_shell(send, 1)
    other = along_shell(pair, 2)
    early, pair = lax.optimization_barrier((early, pair))
    late = call(make_late, shaped((HALF, WIDE), BF16), [], [V])(early)
    late, other = lax.optimization_barrier((late, other))
    scores, stats = call(
        stats_kernel, [shaped((ROWS, HALF), F32), shaped((8, HALF), F32)], [], [V, V]
    )(pair, other)
    all_stats = [stats] + [along_peers(stats, k) for k in (1, 2, 3)]
    probs, evidence = call(
        probs_kernel, [shaped((ROWS, HALF), BF16), shaped((8, HALF), F32)], [], [V] * 5
    )(scores, *all_stats)
    probs_other = along_shell(probs, 1)
    evidence_other = along_shell(evidence, 1)
    sums = call(
        sums_kernel,
        shaped((CLS_PEERS * CHUNK, 128), BF16),
        [V((ROWS, 2 * HALF), BF16), V((CLS, WIDE), F32), V((CLS_PEERS * CHUNK, 128), F32)],
        [V] * 4,
    )(early, late, probs, probs_other)
    own = over_classes(sums)
    new_references = call(
        final_kernel,
        shaped((CYC, OWN_CLASSES, ROW), BF16),
        [V((8 * SLOT, 128), F32)],
        [S, S, V, V],
    )(first, class_offset, own, prior_precision.reshape(1, CYC))
    mine = jnp.where(core == level // 2, evidence[0], evidence_other[0])
    log_evidence = lax.dynamic_slice_in_dim(mine, (level % 2) * OWN_IMAGES, OWN_IMAGES)
    return jnp.transpose(new_references, (1, 0, 2)), log_evidence


def solution(mesh):
    placed = (
        P("img", "shell", None),
        P("img", "shell", None),
        P(),
        P("img"),
        P(None, "shell"),
        P("shell"),
        P("shell"),
    )
    return jax.shard_map(
        local,
        mesh=mesh,
        in_specs=placed,
        out_specs=(P("img", "shell", None), P("img")),
        check_vma=False,
    )
```

```python
import functools

import jax
import jax.numpy as jnp
from jax import lax
from jax.experimental import pallas as pl
from jax.experimental.pallas import tpu as pltpu
from jax.sharding import PartitionSpec as P

ANG = 192
ROT = 48
STEP = ANG // ROT
CYC = 10
ROW = 2 * ANG
TURN = 32
TURNS = ANG // TURN
FINE = TURN // STEP
BLOCK = 2 * CYC * TURN
COEF = TURNS * BLOCK
WIDE = COEF + 128
OWN_IMAGES = 16
OWN_CLASSES = 3
IMG_PEERS = 4
CLS_PEERS = 16
CLS = OWN_CLASSES * CLS_PEERS
TILES = WIDE // 128
SLOT = 32
CHUNK = OWN_CLASSES * SLOT
PITCH = CHUNK + 8
ROWS = TURNS * CLS
HALF = FINE * OWN_IMAGES * 2
F32 = jnp.float32
BF16 = jnp.bfloat16
VMEM_LIMIT = 24 * 1024 * 1024
VMEM_MOST = 60 * 1024 * 1024


def lanes_of(shape):
    return lax.broadcasted_iota(jnp.int32, shape, len(shape) - 1)


def three_parts(x):
    hi = x.astype(BF16).astype(F32)
    rest = x - hi
    mid = rest.astype(BF16).astype(F32)
    return hi, mid, rest - mid


def pick4(lane, parts):
    return jnp.where(
        lane < 64,
        jnp.where(lane < 32, parts[0], parts[1]),
        jnp.where(lane < 96, parts[2], parts[3]),
    )


def turned_tile(rows_of, w, j, lane):
    parts = []
    for t in range(4):
        p, q = 2 * j + t // 2, t % 2
        start = q * ANG + TURN * w
        vreg, off = start // 128, start % 128
        piece = rows_of[p][:, vreg * 128 : vreg * 128 + 128]
        shift = (32 * t - off) % 128
        parts.append(pltpu.roll(piece, shift, 1) if shift else piece)
    return pick4(lane, parts)


def interleaving(back=False):
    a = lax.broadcasted_iota(jnp.int32, (128, 128), 0)
    b = lax.broadcasted_iota(jnp.int32, (128, 128), 1)
    if back:
        a, b = b, a
    return jnp.where(b == (a % TURN) * 4 + a // TURN, 1.0, 0.0).astype(BF16)


def doubled_roll(x, shift):
    lane = lanes_of(x.shape)
    other = pltpu.roll(x, ANG, 1)
    first = lane < ANG
    a0 = pltpu.roll(jnp.where(first, x, other), shift, 1)
    a1 = pltpu.roll(jnp.where(first, other, x), shift, 1)
    return jnp.where(first, a0, a1)


def turn_classes(stacked, shifts):
    row = lax.broadcasted_iota(jnp.int32, stacked.shape, 0) % 8
    turned = doubled_roll(stacked, shifts[0])
    for c in range(1, OWN_CLASSES):
        turned = jnp.where(row == c, doubled_roll(stacked, shifts[c]), turned)
    return turned


def prologue_kernel(
    first_ref, offset_ref, group_ref, images_ref, refs_ref, ctf_ref, noise_ref,
    image_msg, class_msg,
    table_f, table_s, filt, square, stacked, own,
):
    stacked[...] = jnp.zeros_like(stacked)
    for p in range(CYC):
        stacked[p * 8 : p * 8 + OWN_CLASSES, :] = refs_ref[p].astype(F32)
    turned = turn_classes(
        stacked[...], [offset_ref[first_ref[0] + c] for c in range(OWN_CLASSES)]
    )
    rows = [turned[p * 8 : p * 8 + 8] for p in range(CYC)]
    lane8 = lanes_of((8, 128))
    power = jnp.zeros((8, 128), F32)
    for p in range(CYC):
        power = jnp.where(lane8 == p, jnp.sum(rows[p] * rows[p], axis=1, keepdims=True), power)
    mixing = interleaving()
    own[...] = jnp.zeros_like(own)
    for w in range(TURNS):
        tiles = [turned_tile(rows, w, j, lane8) for j in range(5)]
        tiles = jnp.concatenate(tiles, axis=0).astype(BF16)
        tiles = jnp.dot(tiles, mixing, preferred_element_type=F32)
        for j in range(5):
            own[pl.ds(w * 5 + j, OWN_CLASSES, stride=SLOT), :] = tiles[
                j * 8 : j * 8 + OWN_CLASSES
            ]
    hi, mid, lo = three_parts(-0.5 * power)
    extra = hi
    for k, part in enumerate((hi, mid, hi, mid, lo)):
        extra = extra + pltpu.roll(part, 10 * (k + 1), 1)
    own[pl.ds(TILES - 1, OWN_CLASSES, stride=SLOT), :] = extra[:OWN_CLASSES]
    held = own[...].astype(BF16)
    for d in range(CLS_PEERS):
        class_msg[d * CHUNK : (d + 1) * CHUNK, :] = held

    weight = 1.0 / noise_ref[...]
    ctf = ctf_ref[...]
    table_f[...] = jnp.zeros_like(table_f)
    table_s[...] = jnp.zeros_like(table_s)
    table_f[:, :CYC] = ctf * weight
    table_s[:, :CYC] = ctf * ctf * weight
    for i in range(OWN_IMAGES):
        g = group_ref[i]
        filt[i : i + 1, :] = table_f[pl.ds(g, 1), :]
        square[i : i + 1, :] = table_s[pl.ds(g, 1), :]
    lane16 = lanes_of((OWN_IMAGES, 128))
    factors = filt[...]
    rows = []
    for p in range(CYC):
        x = images_ref[p] * factors[:, p : p + 1]
        rows.append(x.astype(BF16).astype(F32))
    for w in range(TURNS):
        tiles = [turned_tile(rows, w, j, lane16) for j in range(5)]
        tiles = jnp.concatenate(tiles, axis=0).astype(BF16)
        tiles = jnp.dot(tiles, mixing, preferred_element_type=F32).astype(BF16)
        for j in range(5):
            at = w * BLOCK + j * 128
            image_msg[:, at : at + 128] = tiles[j * 16 : j * 16 + 16]
    hi, mid, lo = three_parts(square[...])
    extra = hi
    for k, part in enumerate((mid, hi, lo, mid, hi)):
        extra = extra + pltpu.roll(part, 10 * (k + 1), 1)
    image_msg[:, COEF:] = extra.astype(BF16)


def turned_on(cur, nxt, steps):
    s = 4 * STEP * steps
    lane = lanes_of(cur.shape)
    return pltpu.roll(jnp.where(lane >= s, cur, nxt), 128 - s, 1)


def tile_pairs():
    for w in range(TURNS):
        for j in range(5):
            here = w * BLOCK + j * 128
            there = (w + 1) % TURNS * BLOCK + j * 128
            yield slice(here, here + 128), slice(there, there + 128)


def fill_fine(images_ref, fine_ref):
    for rho in range(FINE):
        fine_ref[32 * rho : 32 * rho + 32, COEF:] = images_ref[:, COEF:]
    for here, there in tile_pairs():
        cur, nxt = images_ref[:, here], images_ref[:, there]
        fine_ref[:32, here] = cur
        for rho in range(1, FINE):
            fine_ref[32 * rho : 32 * rho + 32, here] = turned_on(cur, nxt, rho)


def early_kernel(place_ref, f0, f1, f2, f3, fine_ref, rest_ref, mine):
    swapped = place_ref[0] & 1
    near = (place_ref[0] >> 1) == place_ref[1]

    def put(to_ref, pair):
        for k, ref in enumerate(pair):
            at = pl.multiple_of((swapped ^ k) * OWN_IMAGES, 16)
            to_ref[pl.ds(at, OWN_IMAGES), :] = ref[...]

    @pl.when(near)
    def _():
        put(mine, (f0, f1))
        put(rest_ref, (f2, f3))

    @pl.when(jnp.logical_not(near))
    def _():
        put(mine, (f2, f3))
        put(rest_ref, (f0, f1))

    fill_fine(mine, fine_ref)


NT = (((1,), (1,)), ((), ()))


def scores_kernel(
    fine_ref, rest_ref, class_ref, keep_ref, send_ref, fine_rest, wide, stack
):
    for d in range(CLS_PEERS):
        wide[d * PITCH : d * PITCH + CHUNK, :] = class_ref[d * CHUNK : (d + 1) * CHUNK, :].astype(F32)
    for v in range(TILES):
        for c in range(OWN_CLASSES):
            tile = wide[pl.ds(c * SLOT + v, CLS_PEERS, stride=PITCH), :].astype(BF16)
            for g in range(TURNS):
                row = g * CLS + c * CLS_PEERS
                at = v * 128 if v == TILES - 1 else (v * 128 + g * BLOCK) % COEF
                stack[row : row + CLS_PEERS, at : at + 128] = tile
    keep_ref[...] = lax.dot_general(stack[...], fine_ref[...], NT, preferred_element_type=F32)
    fill_fine(rest_ref, fine_rest)
    send_ref[...] = lax.dot_general(
        stack[...], fine_rest[...], NT, preferred_element_type=F32
    )


def over_rotations(op, x):
    for s in (32, 64, 128):
        x = op(x, pltpu.roll(x, s, 1))
    return x


def stats_kernel(mine_ref, other_ref, scores_ref, stats_ref):
    scores = mine_ref[...] + other_ref[...]
    scores_ref[...] = scores
    big = jnp.max(scores, axis=0, keepdims=True)
    big = over_rotations(jnp.maximum, jnp.broadcast_to(big, (8, HALF)))
    part = jnp.sum(jnp.exp(scores - big[:1]), axis=0, keepdims=True)
    part = over_rotations(jnp.add, jnp.broadcast_to(part, (8, HALF)))
    row = lax.broadcasted_iota(jnp.int32, (8, HALF), 0)
    stats_ref[...] = jnp.where(row < 4, big, part)


def probs_kernel(scores_ref, s0, s1, s2, s3, probs_ref, evidence_ref):
    stats = [s[...] for s in (s0, s1, s2, s3)]
    bigs = [s[0:1] for s in stats]
    parts = [s[4:5] for s in stats]
    largest = jnp.maximum(jnp.maximum(bigs[0], bigs[1]), jnp.maximum(bigs[2], bigs[3]))
    total = sum(p * jnp.exp(b - largest) for b, p in zip(bigs, parts))
    evidence = largest + jnp.log(total)
    probs_ref[...] = jnp.exp(scores_ref[...] - evidence).astype(BF16)
    evidence_ref[...] = jnp.broadcast_to(evidence, (8, HALF))


def add_turns(probs_ref, fine_ref, sums, fresh):
    for w in range(0, TURNS, 2):
        span = slice(w * BLOCK, (w + 2) * BLOCK + (128 if w == TURNS - 2 else 0))
        turned = jnp.dot(probs_ref[...], fine_ref[:, span], preferred_element_type=F32)
        for b in (w, w + 1):
            for g in range(TURNS):
                back = (b - g) % TURNS
                at = slice(back * BLOCK, (back + 1) * BLOCK)
                term = turned[g * CLS : (g + 1) * CLS, (b - w) * BLOCK : (b - w + 1) * BLOCK]
                if b == 0 and fresh:
                    sums[:, at] = term
                else:
                    sums[:, at] += term
        if w == TURNS - 2:
            mass = turned[:CLS, 2 * BLOCK :]
            for g in range(1, TURNS):
                mass = mass + turned[g * CLS : (g + 1) * CLS, 2 * BLOCK :]
    return mass


def own_sums_kernel(probs_ref, fine_ref, sums_ref):
    sums_ref[:, COEF:] = add_turns(probs_ref, fine_ref, sums_ref, True)


def all_sums_kernel(probs_ref, fine_ref, own_ref, out_ref, sums, packed):
    sums[...] = own_ref[...]
    mass = sums[:, COEF:] + add_turns(probs_ref, fine_ref, sums, False)
    mass = mass + pltpu.roll(mass, 118, 1) + pltpu.roll(mass, 98, 1)
    mass = jnp.where(lanes_of((CLS, 128)) < CYC, mass, 0.0)
    hi, mid, lo = three_parts(mass)
    sums[:, COEF:] = hi + pltpu.roll(mid, 10, 1) + pltpu.roll(lo, 20, 1)
    for c in range(OWN_CLASSES):
        rows = slice(c * CLS_PEERS, (c + 1) * CLS_PEERS)
        for v in range(SLOT):
            tile = sums[rows, v * 128 : v * 128 + 128] if v < TILES else jnp.zeros((16, 128), F32)
            packed[pl.ds(c * SLOT + v, CLS_PEERS, stride=PITCH), :] = tile
    for d in range(CLS_PEERS):
        out_ref[d * CHUNK : (d + 1) * CHUNK, :] = packed[d * PITCH : d * PITCH + CHUNK, :].astype(BF16)


def final_kernel(offset_ref, msg_ref, prior_ref, out_ref, summed):
    total = msg_ref[:CHUNK, :].astype(F32)
    for d in range(1, CLS_PEERS):
        total = total + msg_ref[d * CHUNK : (d + 1) * CHUNK, :].astype(F32)
    summed[:CHUNK, :] = total
    summed[CHUNK:, :] = jnp.zeros((8 * SLOT - CHUNK, 128), F32)
    lane = lanes_of((8, 128))
    extra = summed[pl.ds(TILES - 1, 8, stride=SLOT), :]
    den = extra + pltpu.roll(extra, 118, 1) + pltpu.roll(extra, 108, 1)
    tiles = {}
    for j in range(5):
        below = []
        for p in (2 * j, 2 * j + 1):
            below.append(den[:, p : p + 1] + prior_ref[0:1, p : p + 1])
        below = jnp.where(lane % 4 < 2, below[0], below[1])
        for w in range(TURNS):
            tiles[w, j] = summed[pl.ds(w * 5 + j, 8, stride=SLOT), :] / below
    keys = list(tiles)
    flat = jnp.concatenate([tiles[k] for k in keys], axis=0).astype(BF16)
    flat = jnp.dot(flat, interleaving(back=True), preferred_element_type=F32)
    tiles = {k: flat[8 * n : 8 * n + 8] for n, k in enumerate(keys)}
    rows = []
    for p in range(CYC):
        vregs = []
        for v in range(3):
            parts = []
            for u in range(4):
                start = 128 * v + 32 * u
                q, w = start // ANG, (start % ANG) // TURN
                t = 2 * (p % 2) + q
                shift = (32 * u - 32 * t) % 128
                piece = tiles[w, p // 2]
                parts.append(pltpu.roll(piece, shift, 1) if shift else piece)
            vregs.append(pick4(lane, parts))
        rows.append(jnp.concatenate(vregs, axis=1))
    shifts = []
    for c in range(OWN_CLASSES):
        off = offset_ref[0, c]
        shifts.append(jnp.where(off == 0, 0, ROW - off))
    turned = turn_classes(jnp.concatenate(rows, axis=0), shifts)
    for p in range(CYC):
        out_ref[p] = turned[p * 8 : p * 8 + OWN_CLASSES].astype(BF16)


def call(kernel, outs, scratch, specs, limit=VMEM_LIMIT, cost=None):
    return pl.pallas_call(
        kernel,
        out_shape=outs,
        in_specs=[pl.BlockSpec(memory_space=s) for s in specs],
        out_specs=jax.tree.map(lambda _: pl.BlockSpec(memory_space=pltpu.VMEM), outs),
        scratch_shapes=scratch,
        compiler_params=pltpu.CompilerParams(vmem_limit_bytes=limit),
        cost_estimate=cost,
    )


S, V = pltpu.SMEM, pltpu.VMEM


def shaped(shape, dtype):
    return jax.ShapeDtypeStruct(shape, dtype)


def local(images, references, class_offset, ctf_group, ctf, noise_power, prior_precision):
    img = lax.axis_index("img")
    core = lax.axis_index("shell") % 2
    level = (img // 4) % 4
    first = (img * OWN_CLASSES).astype(jnp.int32).reshape(1)
    offsets = lax.dynamic_slice_in_dim(class_offset, img * OWN_CLASSES, OWN_CLASSES).reshape(1, -1)
    place = jnp.stack([level, core]).astype(jnp.int32)

    def along_peers(x, k):
        return lax.ppermute(x, "img", [(i, i ^ (4 * k)) for i in range(64)])

    def along_shell(x, k):
        return lax.ppermute(x, "shell", [(i, i ^ k) for i in range(4)])

    groups = [[16 * y + 4 * z + x for y in range(4) for x in range(4)] for z in range(4)]

    def over_classes(x):
        return lax.all_to_all(x, "img", 0, 0, axis_index_groups=groups, tiled=True)

    image_msg, class_msg = call(
        prologue_kernel,
        [shaped((OWN_IMAGES, WIDE), BF16), shaped((CLS_PEERS * CHUNK, 128), BF16)],
        [V((16, 128), F32)] * 4 + [V((CYC * 8, ROW), F32), V((CHUNK, 128), F32)],
        [S, S, S, V, V, V, V],
        VMEM_MOST,
    )(
        first, class_offset, ctf_group, jnp.transpose(images, (1, 0, 2)),
        jnp.transpose(references, (1, 0, 2)), ctf, noise_power.reshape(1, CYC),
    )
    held = [image_msg] + [along_peers(image_msg, k) for k in (1, 2, 3)]
    class_all = over_classes(class_msg)
    fine, rest = call(
        early_kernel,
        [shaped((HALF, WIDE), BF16), shaped((2 * OWN_IMAGES, WIDE), BF16)],
        [V((2 * OWN_IMAGES, WIDE), BF16)],
        [S] + [V] * 4,
        cost=pl.CostEstimate(flops=5 * 10**10, transcendentals=0, bytes_accessed=10**6),
    )(place, *held)
    keep, send, fine_rest = call(
        scores_kernel,
        [shaped((ROWS, HALF), F32)] * 2 + [shaped((HALF, WIDE), BF16)],
        [V((CLS_PEERS * PITCH, 128), F32), V((ROWS, WIDE), BF16)],
        [V, V, V],
    )(fine, rest, class_all)
    pair = keep + along_shell(send, 1)
    other = along_shell(pair, 2)
    scores, stats = call(
        stats_kernel, [shaped((ROWS, HALF), F32), shaped((8, HALF), F32)], [], [V, V]
    )(pair, other)
    all_stats = [stats] + [along_peers(stats, k) for k in (1, 2, 3)]
    probs, evidence = call(
        probs_kernel, [shaped((ROWS, HALF), BF16), shaped((8, HALF), F32)], [], [V] * 5
    )(scores, *all_stats)
    probs_other = along_shell(probs, 1)
    evidence_other = along_shell(evidence, 1)
    own_sums = call(own_sums_kernel, shaped((CLS, WIDE), F32), [], [V, V])(probs, fine)
    sums = call(
        all_sums_kernel,
        shaped((CLS_PEERS * CHUNK, 128), BF16),
        [V((CLS, WIDE), F32), V((CLS_PEERS * PITCH, 128), F32)],
        [V] * 3,
    )(probs_other, fine_rest, own_sums)
    own = over_classes(sums)
    new_references = call(
        final_kernel,
        shaped((CYC, OWN_CLASSES, ROW), BF16),
        [V((8 * SLOT, 128), F32)],
        [V, V, V],
    )(offsets, own, prior_precision.reshape(1, CYC))
    mine = jnp.where(core == level // 2, evidence[0], evidence_other[0])
    log_evidence = lax.dynamic_slice_in_dim(mine, (level % 2) * OWN_IMAGES, OWN_IMAGES)
    return jnp.transpose(new_references, (1, 0, 2)), log_evidence


def solution(mesh):
    placed = (
        P("img", "shell", None),
        P("img", "shell", None),
        P(),
        P("img"),
        P(None, "shell"),
        P("shell"),
        P("shell"),
    )
    return jax.shard_map(
        local,
        mesh=mesh,
        in_specs=placed,
        out_specs=(P("img", "shell", None), P("img")),
        check_vma=False,
    )
```

```python
import functools

import jax
import jax.numpy as jnp
from jax import lax
from jax.experimental import pallas as pl
from jax.experimental.pallas import tpu as pltpu
from jax.sharding import PartitionSpec as P

ANG = 192
ROT = 48
STEP = ANG // ROT
CYC = 10
ROW = 2 * ANG
TURN = 32
TURNS = ANG // TURN
FINE = TURN // STEP
BLOCK = 2 * CYC * TURN
COEF = TURNS * BLOCK
WIDE = COEF + 128
OWN_IMAGES = 16
OWN_CLASSES = 3
IMG_PEERS = 4
CLS_PEERS = 16
CLS = OWN_CLASSES * CLS_PEERS
TILES = WIDE // 128
SLOT = 32
CHUNK = OWN_CLASSES * SLOT
PITCH = CHUNK + 8
ROWS = TURNS * CLS
HALF = FINE * OWN_IMAGES * 2
F32 = jnp.float32
BF16 = jnp.bfloat16
VMEM_LIMIT = 24 * 1024 * 1024
VMEM_MOST = 60 * 1024 * 1024


def lanes_of(shape):
    return lax.broadcasted_iota(jnp.int32, shape, len(shape) - 1)


def three_parts(x):
    hi = x.astype(BF16).astype(F32)
    rest = x - hi
    mid = rest.astype(BF16).astype(F32)
    return hi, mid, rest - mid


def pick4(lane, parts):
    return jnp.where(
        lane < 64,
        jnp.where(lane < 32, parts[0], parts[1]),
        jnp.where(lane < 96, parts[2], parts[3]),
    )


def turned_tile(rows_of, w, j, lane):
    parts = []
    for t in range(4):
        p, q = 2 * j + t // 2, t % 2
        start = q * ANG + TURN * w
        vreg, off = start // 128, start % 128
        piece = rows_of[p][:, vreg * 128 : vreg * 128 + 128]
        shift = (32 * t - off) % 128
        parts.append(pltpu.roll(piece, shift, 1) if shift else piece)
    return pick4(lane, parts)


def interleaving(back=False):
    a = lax.broadcasted_iota(jnp.int32, (128, 128), 0)
    b = lax.broadcasted_iota(jnp.int32, (128, 128), 1)
    if back:
        a, b = b, a
    return jnp.where(b == (a % TURN) * 4 + a // TURN, 1.0, 0.0).astype(BF16)


def doubled_roll(x, shift):
    lane = lanes_of(x.shape)
    other = pltpu.roll(x, ANG, 1)
    first = lane < ANG
    a0 = pltpu.roll(jnp.where(first, x, other), shift, 1)
    a1 = pltpu.roll(jnp.where(first, other, x), shift, 1)
    return jnp.where(first, a0, a1)


def turn_classes(stacked, shifts):
    row = lax.broadcasted_iota(jnp.int32, stacked.shape, 0) % 8
    turned = doubled_roll(stacked, shifts[0])
    for c in range(1, OWN_CLASSES):
        turned = jnp.where(row == c, doubled_roll(stacked, shifts[c]), turned)
    return turned


def prologue_kernel(
    first_ref, offset_ref, group_ref, images_ref, refs_ref, ctf_ref, noise_ref,
    image_msg, class_msg,
    table_f, table_s, filt, square, stacked, own,
):
    stacked[...] = jnp.zeros_like(stacked)
    for p in range(CYC):
        stacked[p * 8 : p * 8 + OWN_CLASSES, :] = refs_ref[p].astype(F32)
    turned = turn_classes(
        stacked[...], [offset_ref[first_ref[0] + c] for c in range(OWN_CLASSES)]
    )
    rows = [turned[p * 8 : p * 8 + 8] for p in range(CYC)]
    lane8 = lanes_of((8, 128))
    power = jnp.zeros((8, 128), F32)
    for p in range(CYC):
        power = jnp.where(lane8 == p, jnp.sum(rows[p] * rows[p], axis=1, keepdims=True), power)
    mixing = interleaving()
    own[...] = jnp.zeros_like(own)
    for w in range(TURNS):
        tiles = [turned_tile(rows, w, j, lane8) for j in range(5)]
        tiles = jnp.concatenate(tiles, axis=0).astype(BF16)
        tiles = jnp.dot(tiles, mixing, preferred_element_type=F32)
        for j in range(5):
            own[pl.ds(w * 5 + j, OWN_CLASSES, stride=SLOT), :] = tiles[
                j * 8 : j * 8 + OWN_CLASSES
            ]
    hi, mid, lo = three_parts(-0.5 * power)
    extra = hi
    for k, part in enumerate((hi, mid, hi, mid, lo)):
        extra = extra + pltpu.roll(part, 10 * (k + 1), 1)
    own[pl.ds(TILES - 1, OWN_CLASSES, stride=SLOT), :] = extra[:OWN_CLASSES]
    held = own[...].astype(BF16)
    for d in range(CLS_PEERS):
        class_msg[d * CHUNK : (d + 1) * CHUNK, :] = held

    weight = 1.0 / noise_ref[...]
    ctf = ctf_ref[...]
    table_f[...] = jnp.zeros_like(table_f)
    table_s[...] = jnp.zeros_like(table_s)
    table_f[:, :CYC] = ctf * weight
    table_s[:, :CYC] = ctf * ctf * weight
    for i in range(OWN_IMAGES):
        g = group_ref[i]
        filt[i : i + 1, :] = table_f[pl.ds(g, 1), :]
        square[i : i + 1, :] = table_s[pl.ds(g, 1), :]
    lane16 = lanes_of((OWN_IMAGES, 128))
    factors = filt[...]
    rows = []
    for p in range(CYC):
        x = images_ref[p] * factors[:, p : p + 1]
        rows.append(x.astype(BF16).astype(F32))
    for w in range(TURNS):
        tiles = [turned_tile(rows, w, j, lane16) for j in range(5)]
        tiles = jnp.concatenate(tiles, axis=0).astype(BF16)
        tiles = jnp.dot(tiles, mixing, preferred_element_type=F32).astype(BF16)
        for j in range(5):
            at = w * BLOCK + j * 128
            image_msg[:, at : at + 128] = tiles[j * 16 : j * 16 + 16]
    hi, mid, lo = three_parts(square[...])
    extra = hi
    for k, part in enumerate((mid, hi, lo, mid, hi)):
        extra = extra + pltpu.roll(part, 10 * (k + 1), 1)
    image_msg[:, COEF:] = extra.astype(BF16)


def turned_on(cur, nxt, steps):
    s = 4 * STEP * steps
    lane = lanes_of(cur.shape)
    return pltpu.roll(jnp.where(lane >= s, cur, nxt), 128 - s, 1)


def tile_pairs():
    for w in range(TURNS):
        for j in range(5):
            here = w * BLOCK + j * 128
            there = (w + 1) % TURNS * BLOCK + j * 128
            yield slice(here, here + 128), slice(there, there + 128)


def fill_fine(images_ref, fine_ref):
    for rho in range(FINE):
        fine_ref[32 * rho : 32 * rho + 32, COEF:] = images_ref[:, COEF:]
    for here, there in tile_pairs():
        cur, nxt = images_ref[:, here], images_ref[:, there]
        fine_ref[:32, here] = cur
        for rho in range(1, FINE):
            fine_ref[32 * rho : 32 * rho + 32, here] = turned_on(cur, nxt, rho)


def place():
    return lax.axis_index("img") // IMG_PEERS % IMG_PEERS, lax.axis_index("shell") % 2


def gather_pair(pair, to_ref):
    level, _ = place()
    for k, ref in enumerate(pair):
        at = pl.multiple_of(((level & 1) ^ k) * OWN_IMAGES, 16)
        to_ref[pl.ds(at, OWN_IMAGES), :] = ref[...]


def early_kernel(f2, f3, fine_ref, pair):
    gather_pair((f2, f3), pair)
    fill_fine(pair, fine_ref)


def is_near():
    level, core = place()
    return (level >> 1) == core


NT = (((1,), (1,)), ((), ()))


def scores_kernel(
    far_ref, f0, f1, class_ref, keep_ref, send_ref, fine_ref, pair, wide, stack, part
):
    gather_pair((f0, f1), pair)
    for d in range(CLS_PEERS):
        wide[d * PITCH : d * PITCH + CHUNK, :] = class_ref[d * CHUNK : (d + 1) * CHUNK, :].astype(F32)
    for v in range(TILES):
        for c in range(OWN_CLASSES):
            tile = wide[pl.ds(c * SLOT + v, CLS_PEERS, stride=PITCH), :].astype(BF16)
            for g in range(TURNS):
                row = g * CLS + c * CLS_PEERS
                at = v * 128 if v == TILES - 1 else (v * 128 + g * BLOCK) % COEF
                stack[row : row + CLS_PEERS, at : at + 128] = tile
    part[...] = lax.dot_general(stack[...], far_ref[...], NT, preferred_element_type=F32)
    fill_fine(pair, fine_ref.at[0])
    fine_ref[1] = far_ref[...]
    last = lax.dot_general(stack[...], fine_ref[0], NT, preferred_element_type=F32)
    first = part[...]
    near = is_near()
    keep_ref[...] = jnp.where(near, last, first)
    send_ref[...] = jnp.where(near, first, last)


def over_rotations(op, x):
    for s in (32, 64, 128):
        x = op(x, pltpu.roll(x, s, 1))
    return x


def stats_kernel(mine_ref, other_ref, scores_ref, stats_ref):
    scores = mine_ref[...] + other_ref[...]
    scores_ref[...] = scores
    big = jnp.max(scores, axis=0, keepdims=True)
    big = over_rotations(jnp.maximum, jnp.broadcast_to(big, (8, HALF)))
    part = jnp.sum(jnp.exp(scores - big[:1]), axis=0, keepdims=True)
    part = over_rotations(jnp.add, jnp.broadcast_to(part, (8, HALF)))
    row = lax.broadcasted_iota(jnp.int32, (8, HALF), 0)
    stats_ref[...] = jnp.where(row < 4, big, part)


def probs_kernel(scores_ref, s0, s1, s2, s3, probs_ref, evidence_ref):
    stats = [s[...] for s in (s0, s1, s2, s3)]
    bigs = [s[0:1] for s in stats]
    parts = [s[4:5] for s in stats]
    largest = jnp.maximum(jnp.maximum(bigs[0], bigs[1]), jnp.maximum(bigs[2], bigs[3]))
    total = sum(p * jnp.exp(b - largest) for b, p in zip(bigs, parts))
    evidence = largest + jnp.log(total)
    probs_ref[...] = jnp.exp(scores_ref[...] - evidence).astype(BF16)
    evidence_ref[...] = jnp.broadcast_to(evidence, (8, HALF))


def add_turns(probs_ref, fine_ref, sums, fresh):
    for w in range(0, TURNS, 2):
        span = slice(w * BLOCK, (w + 2) * BLOCK + (128 if w == TURNS - 2 else 0))
        turned = jnp.dot(probs_ref[...], fine_ref[:, span], preferred_element_type=F32)
        for b in (w, w + 1):
            for g in range(TURNS):
                back = (b - g) % TURNS
                at = slice(back * BLOCK, (back + 1) * BLOCK)
                term = turned[g * CLS : (g + 1) * CLS, (b - w) * BLOCK : (b - w + 1) * BLOCK]
                if b == 0 and fresh:
                    sums[:, at] = term
                else:
                    sums[:, at] += term
        if w == TURNS - 2:
            mass = turned[:CLS, 2 * BLOCK :]
            for g in range(1, TURNS):
                mass = mass + turned[g * CLS : (g + 1) * CLS, 2 * BLOCK :]
    return mass


def own_sums_kernel(probs_ref, fine_ref, sums_ref):
    mine = fine_ref.at[jnp.where(is_near(), 0, 1)]
    sums_ref[:, COEF:] = add_turns(probs_ref, mine, sums_ref, True)


def all_sums_kernel(probs_ref, fine_ref, own_ref, out_ref, sums, packed):
    sums[...] = own_ref[...]
    rest = fine_ref.at[jnp.where(is_near(), 1, 0)]
    mass = sums[:, COEF:] + add_turns(probs_ref, rest, sums, False)
    mass = mass + pltpu.roll(mass, 118, 1) + pltpu.roll(mass, 98, 1)
    mass = jnp.where(lanes_of((CLS, 128)) < CYC, mass, 0.0)
    hi, mid, lo = three_parts(mass)
    sums[:, COEF:] = hi + pltpu.roll(mid, 10, 1) + pltpu.roll(lo, 20, 1)
    for c in range(OWN_CLASSES):
        rows = slice(c * CLS_PEERS, (c + 1) * CLS_PEERS)
        for v in range(SLOT):
            tile = sums[rows, v * 128 : v * 128 + 128] if v < TILES else jnp.zeros((16, 128), F32)
            packed[pl.ds(c * SLOT + v, CLS_PEERS, stride=PITCH), :] = tile
    for d in range(CLS_PEERS):
        out_ref[d * CHUNK : (d + 1) * CHUNK, :] = packed[d * PITCH : d * PITCH + CHUNK, :].astype(BF16)


def final_kernel(offset_ref, msg_ref, prior_ref, out_ref, summed):
    total = msg_ref[:CHUNK, :].astype(F32)
    for d in range(1, CLS_PEERS):
        total = total + msg_ref[d * CHUNK : (d + 1) * CHUNK, :].astype(F32)
    summed[:CHUNK, :] = total
    summed[CHUNK:, :] = jnp.zeros((8 * SLOT - CHUNK, 128), F32)
    lane = lanes_of((8, 128))
    extra = summed[pl.ds(TILES - 1, 8, stride=SLOT), :]
    den = extra + pltpu.roll(extra, 118, 1) + pltpu.roll(extra, 108, 1)
    tiles = {}
    for j in range(5):
        below = []
        for p in (2 * j, 2 * j + 1):
            below.append(den[:, p : p + 1] + prior_ref[0:1, p : p + 1])
        below = jnp.where(lane % 4 < 2, below[0], below[1])
        for w in range(TURNS):
            tiles[w, j] = summed[pl.ds(w * 5 + j, 8, stride=SLOT), :] / below
    keys = list(tiles)
    flat = jnp.concatenate([tiles[k] for k in keys], axis=0).astype(BF16)
    flat = jnp.dot(flat, interleaving(back=True), preferred_element_type=F32)
    tiles = {k: flat[8 * n : 8 * n + 8] for n, k in enumerate(keys)}
    rows = []
    for p in range(CYC):
        vregs = []
        for v in range(3):
            parts = []
            for u in range(4):
                start = 128 * v + 32 * u
                q, w = start // ANG, (start % ANG) // TURN
                t = 2 * (p % 2) + q
                shift = (32 * u - 32 * t) % 128
                piece = tiles[w, p // 2]
                parts.append(pltpu.roll(piece, shift, 1) if shift else piece)
            vregs.append(pick4(lane, parts))
        rows.append(jnp.concatenate(vregs, axis=1))
    shifts = []
    for c in range(OWN_CLASSES):
        off = offset_ref[0, c]
        shifts.append(jnp.where(off == 0, 0, ROW - off))
    turned = turn_classes(jnp.concatenate(rows, axis=0), shifts)
    for p in range(CYC):
        out_ref[p] = turned[p * 8 : p * 8 + OWN_CLASSES].astype(BF16)


def call(kernel, outs, scratch, specs, limit=VMEM_LIMIT, cost=None):
    return pl.pallas_call(
        kernel,
        out_shape=outs,
        in_specs=[pl.BlockSpec(memory_space=s) for s in specs],
        out_specs=jax.tree.map(lambda _: pl.BlockSpec(memory_space=pltpu.VMEM), outs),
        scratch_shapes=scratch,
        compiler_params=pltpu.CompilerParams(vmem_limit_bytes=limit),
        cost_estimate=cost,
    )


S, V = pltpu.SMEM, pltpu.VMEM


def shaped(shape, dtype):
    return jax.ShapeDtypeStruct(shape, dtype)


def local(images, references, class_offset, ctf_group, ctf, noise_power, prior_precision):
    img = lax.axis_index("img")
    level, core = place()
    first = (img * OWN_CLASSES).astype(jnp.int32).reshape(1)
    offsets = lax.dynamic_slice_in_dim(class_offset, img * OWN_CLASSES, OWN_CLASSES).reshape(1, -1)

    def along_peers(x, k):
        return lax.ppermute(x, "img", [(i, i ^ (4 * k)) for i in range(64)])

    def along_shell(x, k):
        return lax.ppermute(x, "shell", [(i, i ^ k) for i in range(4)])

    groups = [[16 * y + 4 * z + x for y in range(4) for x in range(4)] for z in range(4)]

    def over_classes(x):
        return lax.all_to_all(x, "img", 0, 0, axis_index_groups=groups, tiled=True)

    image_msg, class_msg = call(
        prologue_kernel,
        [shaped((OWN_IMAGES, WIDE), BF16), shaped((CLS_PEERS * CHUNK, 128), BF16)],
        [V((16, 128), F32)] * 4 + [V((CYC * 8, ROW), F32), V((CHUNK, 128), F32)],
        [S, S, S, V, V, V, V],
        VMEM_MOST,
    )(
        first, class_offset, ctf_group, jnp.transpose(images, (1, 0, 2)),
        jnp.transpose(references, (1, 0, 2)), ctf, noise_power.reshape(1, CYC),
    )
    held = [image_msg] + [along_peers(image_msg, k) for k in (1, 2, 3)]
    class_all = over_classes(class_msg)
    far = call(
        early_kernel,
        shaped((HALF, WIDE), BF16),
        [V((2 * OWN_IMAGES, WIDE), BF16)],
        [V, V],
        cost=pl.CostEstimate(flops=26 * 10**8, transcendentals=0, bytes_accessed=10**6),
    )(held[2], held[3])
    keep, send, fine = call(
        scores_kernel,
        [shaped((ROWS, HALF), F32)] * 2 + [shaped((2, HALF, WIDE), BF16)],
        [
            V((2 * OWN_IMAGES, WIDE), BF16), V((CLS_PEERS * PITCH, 128), F32),
            V((ROWS, WIDE), BF16), V((ROWS, HALF), F32),
        ],
        [V] * 4,
    )(far, held[0], held[1], class_all)
    pair = keep + along_shell(send, 1)
    other = along_shell(pair, 2)
    scores, stats = call(
        stats_kernel, [shaped((ROWS, HALF), F32), shaped((8, HALF), F32)], [], [V, V]
    )(pair, other)
    all_stats = [stats] + [along_peers(stats, k) for k in (1, 2, 3)]
    probs, evidence = call(
        probs_kernel, [shaped((ROWS, HALF), BF16), shaped((8, HALF), F32)], [], [V] * 5
    )(scores, *all_stats)
    probs_other = along_shell(probs, 1)
    evidence_other = along_shell(evidence, 1)
    own_sums = call(own_sums_kernel, shaped((CLS, WIDE), F32), [], [V, V])(probs, fine)
    sums = call(
        all_sums_kernel,
        shaped((CLS_PEERS * CHUNK, 128), BF16),
        [V((CLS, WIDE), F32), V((CLS_PEERS * PITCH, 128), F32)],
        [V] * 3,
    )(probs_other, fine, own_sums)
    own = over_classes(sums)
    new_references = call(
        final_kernel,
        shaped((CYC, OWN_CLASSES, ROW), BF16),
        [V((8 * SLOT, 128), F32)],
        [V, V, V],
    )(offsets, own, prior_precision.reshape(1, CYC))
    mine = jnp.where(core == level // 2, evidence[0], evidence_other[0])
    log_evidence = lax.dynamic_slice_in_dim(mine, (level % 2) * OWN_IMAGES, OWN_IMAGES)
    return jnp.transpose(new_references, (1, 0, 2)), log_evidence


def solution(mesh):
    placed = (
        P("img", "shell", None),
        P("img", "shell", None),
        P(),
        P("img"),
        P(None, "shell"),
        P("shell"),
        P("shell"),
    )
    return jax.shard_map(
        local,
        mesh=mesh,
        in_specs=placed,
        out_specs=(P("img", "shell", None), P("img")),
        check_vma=False,
    )
```

```python
import functools

import jax
import jax.numpy as jnp
from jax import lax
from jax.experimental import pallas as pl
from jax.experimental.pallas import tpu as pltpu
from jax.sharding import PartitionSpec as P

ANG = 192
ROT = 48
STEP = ANG // ROT
CYC = 10
ROW = 2 * ANG
TURN = 32
TURNS = ANG // TURN
FINE = TURN // STEP
BLOCK = 2 * CYC * TURN
COEF = TURNS * BLOCK
WIDE = COEF + 128
OWN_IMAGES = 16
OWN_CLASSES = 3
IMG_PEERS = 4
CLS_PEERS = 16
CLS = OWN_CLASSES * CLS_PEERS
TILES = WIDE // 128
SLOT = 32
CHUNK = OWN_CLASSES * SLOT
PITCH = CHUNK + 8
ROWS = TURNS * CLS
HALF = FINE * OWN_IMAGES * 2
F32 = jnp.float32
BF16 = jnp.bfloat16
VMEM_LIMIT = 24 * 1024 * 1024
VMEM_MOST = 60 * 1024 * 1024


def lanes_of(shape):
    return lax.broadcasted_iota(jnp.int32, shape, len(shape) - 1)


def three_parts(x):
    hi = x.astype(BF16).astype(F32)
    rest = x - hi
    mid = rest.astype(BF16).astype(F32)
    return hi, mid, rest - mid


def pick4(lane, parts):
    return jnp.where(
        lane < 64,
        jnp.where(lane < 32, parts[0], parts[1]),
        jnp.where(lane < 96, parts[2], parts[3]),
    )


def turned_tile(rows_of, w, j, lane):
    parts = []
    for t in range(4):
        p, q = 2 * j + t // 2, t % 2
        start = q * ANG + TURN * w
        vreg, off = start // 128, start % 128
        piece = rows_of[p][:, vreg * 128 : vreg * 128 + 128]
        shift = (32 * t - off) % 128
        parts.append(pltpu.roll(piece, shift, 1) if shift else piece)
    return pick4(lane, parts)


def interleaving(back=False):
    a = lax.broadcasted_iota(jnp.int32, (128, 128), 0)
    b = lax.broadcasted_iota(jnp.int32, (128, 128), 1)
    if back:
        a, b = b, a
    return jnp.where(b == (a % TURN) * 4 + a // TURN, 1.0, 0.0).astype(BF16)


def doubled_roll(x, shift):
    lane = lanes_of(x.shape)
    other = pltpu.roll(x, ANG, 1)
    first = lane < ANG
    a0 = pltpu.roll(jnp.where(first, x, other), shift, 1)
    a1 = pltpu.roll(jnp.where(first, other, x), shift, 1)
    return jnp.where(first, a0, a1)


LANES = [slice(v * 128, v * 128 + 128) for v in range(ROW // 128)]
STEP_ROWS = 24


def turn_classes(grouped, shifts):
    for c, shift in enumerate(shifts):
        rows = slice(c * STEP_ROWS, c * STEP_ROWS + 16)
        wide = jnp.concatenate([grouped[v, rows, :] for v in range(3)], axis=1)
        wide = doubled_roll(wide, shift)
        for v, at in enumerate(LANES):
            grouped[v, rows, :] = wide[:, at]


def prologue_kernel(
    first_ref, offset_ref, group_ref, images_ref, refs_ref, ctf_ref, noise_ref,
    image_msg, class_msg,
    table_f, table_s, filt, square, grouped, own,
):
    grouped[...] = jnp.zeros_like(grouped)
    for p in range(CYC):
        row = refs_ref[p].astype(F32)
        for v, at in enumerate(LANES):
            grouped[v, pl.ds(p, OWN_CLASSES, stride=STEP_ROWS), :] = row[:, at]
    turn_classes(grouped, [offset_ref[first_ref[0] + c] for c in range(OWN_CLASSES)])
    rows = []
    for p in range(CYC):
        parts = [grouped[v, pl.ds(p, 8, stride=STEP_ROWS), :] for v in range(3)]
        rows.append(jnp.concatenate(parts, axis=1))
    lane8 = lanes_of((8, 128))
    power = jnp.zeros((8, 128), F32)
    for p in range(CYC):
        power = jnp.where(lane8 == p, jnp.sum(rows[p] * rows[p], axis=1, keepdims=True), power)
    mixing = interleaving()
    own[...] = jnp.zeros_like(own)
    for w in range(TURNS):
        tiles = [turned_tile(rows, w, j, lane8) for j in range(5)]
        tiles = jnp.concatenate(tiles, axis=0).astype(BF16)
        tiles = jnp.dot(tiles, mixing, preferred_element_type=F32)
        for j in range(5):
            own[pl.ds(w * 5 + j, OWN_CLASSES, stride=SLOT), :] = tiles[
                j * 8 : j * 8 + OWN_CLASSES
            ]
    hi, mid, lo = three_parts(-0.5 * power)
    extra = hi
    for k, part in enumerate((hi, mid, hi, mid, lo)):
        extra = extra + pltpu.roll(part, 10 * (k + 1), 1)
    own[pl.ds(TILES - 1, OWN_CLASSES, stride=SLOT), :] = extra[:OWN_CLASSES]
    held = own[...].astype(BF16)
    for d in range(CLS_PEERS):
        class_msg[d * CHUNK : (d + 1) * CHUNK, :] = held

    weight = 1.0 / noise_ref[...]
    ctf = ctf_ref[...]
    table_f[...] = jnp.zeros_like(table_f)
    table_s[...] = jnp.zeros_like(table_s)
    table_f[:, :CYC] = ctf * weight
    table_s[:, :CYC] = ctf * ctf * weight
    for i in range(OWN_IMAGES):
        g = group_ref[i]
        filt[i : i + 1, :] = table_f[pl.ds(g, 1), :]
        square[i : i + 1, :] = table_s[pl.ds(g, 1), :]
    lane16 = lanes_of((OWN_IMAGES, 128))
    factors = filt[...]
    rows = []
    for p in range(CYC):
        x = images_ref[p] * factors[:, p : p + 1]
        rows.append(x.astype(BF16).astype(F32))
    for w in range(TURNS):
        tiles = [turned_tile(rows, w, j, lane16) for j in range(5)]
        tiles = jnp.concatenate(tiles, axis=0).astype(BF16)
        tiles = jnp.dot(tiles, mixing, preferred_element_type=F32).astype(BF16)
        for j in range(5):
            at = w * BLOCK + j * 128
            image_msg[:, at : at + 128] = tiles[j * 16 : j * 16 + 16]
    hi, mid, lo = three_parts(square[...])
    extra = hi
    for k, part in enumerate((mid, hi, lo, mid, hi)):
        extra = extra + pltpu.roll(part, 10 * (k + 1), 1)
    image_msg[:, COEF:] = extra.astype(BF16)


def turned_on(cur, nxt, steps):
    s = 4 * STEP * steps
    lane = lanes_of(cur.shape)
    return pltpu.roll(jnp.where(lane >= s, cur, nxt), 128 - s, 1)


def tile_pairs():
    for w in range(TURNS):
        for j in range(5):
            here = w * BLOCK + j * 128
            there = (w + 1) % TURNS * BLOCK + j * 128
            yield slice(here, here + 128), slice(there, there + 128)


def fill_fine(images_ref, fine_ref):
    for rho in range(FINE):
        fine_ref[32 * rho : 32 * rho + 32, COEF:] = images_ref[:, COEF:]
    for here, there in tile_pairs():
        cur, nxt = images_ref[:, here], images_ref[:, there]
        fine_ref[:32, here] = cur
        for rho in range(1, FINE):
            fine_ref[32 * rho : 32 * rho + 32, here] = turned_on(cur, nxt, rho)


def place():
    return lax.axis_index("img") // IMG_PEERS % IMG_PEERS, lax.axis_index("shell") % 2


def gather_pair(pair, to_ref):
    level, _ = place()
    for k, ref in enumerate(pair):
        at = pl.multiple_of(((level & 1) ^ k) * OWN_IMAGES, 16)
        to_ref[pl.ds(at, OWN_IMAGES), :] = ref[...]


def early_kernel(f2, f3, fine_ref, pair):
    gather_pair((f2, f3), pair)
    fill_fine(pair, fine_ref)


def is_near():
    level, core = place()
    return (level >> 1) == core


NT = (((1,), (1,)), ((), ()))


def scores_kernel(
    far_ref, f0, f1, class_ref, keep_ref, send_ref, fine_ref, pair, wide, stack, part
):
    gather_pair((f0, f1), pair)
    for d in range(CLS_PEERS):
        wide[d * PITCH : d * PITCH + CHUNK, :] = class_ref[d * CHUNK : (d + 1) * CHUNK, :].astype(F32)
    for v in range(TILES):
        for c in range(OWN_CLASSES):
            tile = wide[pl.ds(c * SLOT + v, CLS_PEERS, stride=PITCH), :].astype(BF16)
            for g in range(TURNS):
                row = g * CLS + c * CLS_PEERS
                at = v * 128 if v == TILES - 1 else (v * 128 + g * BLOCK) % COEF
                stack[row : row + CLS_PEERS, at : at + 128] = tile
    part[...] = lax.dot_general(stack[...], far_ref[...], NT, preferred_element_type=F32)
    fill_fine(pair, fine_ref.at[0])
    fine_ref[1] = far_ref[...]
    last = lax.dot_general(stack[...], fine_ref[0], NT, preferred_element_type=F32)
    first = part[...]
    near = is_near()
    keep_ref[...] = jnp.where(near, last, first)
    send_ref[...] = jnp.where(near, first, last)


def over_rotations(op, x):
    for s in (32, 64, 128):
        x = op(x, pltpu.roll(x, s, 1))
    return x


def stats_kernel(mine_ref, other_ref, scores_ref, stats_ref):
    scores = mine_ref[...] + other_ref[...]
    scores_ref[...] = scores
    big = jnp.max(scores, axis=0, keepdims=True)
    big = over_rotations(jnp.maximum, jnp.broadcast_to(big, (8, HALF)))
    part = jnp.sum(jnp.exp(scores - big[:1]), axis=0, keepdims=True)
    part = over_rotations(jnp.add, jnp.broadcast_to(part, (8, HALF)))
    row = lax.broadcasted_iota(jnp.int32, (8, HALF), 0)
    stats_ref[...] = jnp.where(row < 4, big, part)


def probs_kernel(scores_ref, s0, s1, s2, s3, probs_ref, evidence_ref):
    stats = [s[...] for s in (s0, s1, s2, s3)]
    bigs = [s[0:1] for s in stats]
    parts = [s[4:5] for s in stats]
    largest = jnp.maximum(jnp.maximum(bigs[0], bigs[1]), jnp.maximum(bigs[2], bigs[3]))
    total = sum(p * jnp.exp(b - largest) for b, p in zip(bigs, parts))
    evidence = largest + jnp.log(total)
    probs_ref[...] = jnp.exp(scores_ref[...] - evidence).astype(BF16)
    evidence_ref[...] = jnp.broadcast_to(evidence, (8, HALF))


def add_turns(probs_ref, fine_ref, sums, base):
    for w in range(0, TURNS, 2):
        span = slice(w * BLOCK, (w + 2) * BLOCK + (128 if w == TURNS - 2 else 0))
        turned = jnp.dot(probs_ref[...], fine_ref[:, span], preferred_element_type=F32)
        for b in (w, w + 1):
            for g in range(TURNS):
                back = (b - g) % TURNS
                at = slice(back * BLOCK, (back + 1) * BLOCK)
                term = turned[g * CLS : (g + 1) * CLS, (b - w) * BLOCK : (b - w + 1) * BLOCK]
                if b == 0:
                    sums[:, at] = term if base is None else base[:, at] + term
                else:
                    sums[:, at] += term
        if w == TURNS - 2:
            mass = turned[:CLS, 2 * BLOCK :]
            for g in range(1, TURNS):
                mass = mass + turned[g * CLS : (g + 1) * CLS, 2 * BLOCK :]
    return mass


def own_sums_kernel(probs_ref, fine_ref, sums_ref):
    mine = fine_ref.at[jnp.where(is_near(), 0, 1)]
    sums_ref[:, COEF:] = add_turns(probs_ref, mine, sums_ref, None)


def all_sums_kernel(probs_ref, fine_ref, own_ref, out_ref, sums, packed):
    rest = fine_ref.at[jnp.where(is_near(), 1, 0)]
    mass = own_ref[:, COEF:] + add_turns(probs_ref, rest, sums, own_ref)
    mass = mass + pltpu.roll(mass, 118, 1) + pltpu.roll(mass, 98, 1)
    mass = jnp.where(lanes_of((CLS, 128)) < CYC, mass, 0.0)
    hi, mid, lo = three_parts(mass)
    sums[:, COEF:] = hi + pltpu.roll(mid, 10, 1) + pltpu.roll(lo, 20, 1)
    for c in range(OWN_CLASSES):
        rows = slice(c * CLS_PEERS, (c + 1) * CLS_PEERS)
        for v in range(SLOT):
            tile = sums[rows, v * 128 : v * 128 + 128] if v < TILES else jnp.zeros((16, 128), F32)
            packed[pl.ds(c * SLOT + v, CLS_PEERS, stride=PITCH), :] = tile
    for d in range(CLS_PEERS):
        out_ref[d * CHUNK : (d + 1) * CHUNK, :] = packed[d * PITCH : d * PITCH + CHUNK, :].astype(BF16)


def final_kernel(offset_ref, msg_ref, prior_ref, out_ref, summed, grouped):
    total = msg_ref[:CHUNK, :].astype(F32)
    for d in range(1, CLS_PEERS):
        total = total + msg_ref[d * CHUNK : (d + 1) * CHUNK, :].astype(F32)
    summed[:CHUNK, :] = total
    summed[CHUNK:, :] = jnp.zeros((8 * SLOT - CHUNK, 128), F32)
    lane = lanes_of((8, 128))
    extra = summed[pl.ds(TILES - 1, 8, stride=SLOT), :]
    den = extra + pltpu.roll(extra, 118, 1) + pltpu.roll(extra, 108, 1)
    tiles = {}
    for j in range(5):
        below = []
        for p in (2 * j, 2 * j + 1):
            below.append(den[:, p : p + 1] + prior_ref[0:1, p : p + 1])
        below = jnp.where(lane % 4 < 2, below[0], below[1])
        for w in range(TURNS):
            tiles[w, j] = summed[pl.ds(w * 5 + j, 8, stride=SLOT), :] / below
    keys = list(tiles)
    flat = jnp.concatenate([tiles[k] for k in keys], axis=0).astype(BF16)
    flat = jnp.dot(flat, interleaving(back=True), preferred_element_type=F32)
    tiles = {k: flat[8 * n : 8 * n + 8] for n, k in enumerate(keys)}
    grouped[...] = jnp.zeros_like(grouped)
    for p in range(CYC):
        for v in range(3):
            parts = []
            for u in range(4):
                start = 128 * v + 32 * u
                q, w = start // ANG, (start % ANG) // TURN
                t = 2 * (p % 2) + q
                shift = (32 * u - 32 * t) % 128
                piece = tiles[w, p // 2]
                parts.append(pltpu.roll(piece, shift, 1) if shift else piece)
            grouped[v, pl.ds(p, OWN_CLASSES, stride=STEP_ROWS), :] = pick4(lane, parts)[
                :OWN_CLASSES
            ]
    shifts = []
    for c in range(OWN_CLASSES):
        off = offset_ref[0, c]
        shifts.append(jnp.where(off == 0, 0, ROW - off))
    turn_classes(grouped, shifts)
    for p in range(CYC):
        for v, at in enumerate(LANES):
            out_ref[p, :, at] = grouped[v, pl.ds(p, OWN_CLASSES, stride=STEP_ROWS), :].astype(BF16)


def call(kernel, outs, scratch, specs, limit=VMEM_LIMIT, cost=None):
    return pl.pallas_call(
        kernel,
        out_shape=outs,
        in_specs=[pl.BlockSpec(memory_space=s) for s in specs],
        out_specs=jax.tree.map(lambda _: pl.BlockSpec(memory_space=pltpu.VMEM), outs),
        scratch_shapes=scratch,
        compiler_params=pltpu.CompilerParams(vmem_limit_bytes=limit),
        cost_estimate=cost,
    )


S, V = pltpu.SMEM, pltpu.VMEM


def shaped(shape, dtype):
    return jax.ShapeDtypeStruct(shape, dtype)


def local(images, references, class_offset, ctf_group, ctf, noise_power, prior_precision):
    img = lax.axis_index("img")
    level, core = place()
    first = (img * OWN_CLASSES).astype(jnp.int32).reshape(1)
    offsets = lax.dynamic_slice_in_dim(class_offset, img * OWN_CLASSES, OWN_CLASSES).reshape(1, -1)

    def along_peers(x, k):
        return lax.ppermute(x, "img", [(i, i ^ (4 * k)) for i in range(64)])

    def along_shell(x, k):
        return lax.ppermute(x, "shell", [(i, i ^ k) for i in range(4)])

    groups = [[16 * y + 4 * z + x for y in range(4) for x in range(4)] for z in range(4)]

    def over_classes(x):
        return lax.all_to_all(x, "img", 0, 0, axis_index_groups=groups, tiled=True)

    image_msg, class_msg = call(
        prologue_kernel,
        [shaped((OWN_IMAGES, WIDE), BF16), shaped((CLS_PEERS * CHUNK, 128), BF16)],
        [V((16, 128), F32)] * 4 + [V((3, 8 * STEP_ROWS, 128), F32), V((CHUNK, 128), F32)],
        [S, S, S, V, V, V, V],
        VMEM_MOST,
    )(
        first, class_offset, ctf_group, jnp.transpose(images, (1, 0, 2)),
        jnp.transpose(references, (1, 0, 2)), ctf, noise_power.reshape(1, CYC),
    )
    held = [image_msg] + [along_peers(image_msg, k) for k in (1, 2, 3)]
    class_all = over_classes(class_msg)
    far = call(
        early_kernel,
        shaped((HALF, WIDE), BF16),
        [V((2 * OWN_IMAGES, WIDE), BF16)],
        [V, V],
        cost=pl.CostEstimate(flops=26 * 10**8, transcendentals=0, bytes_accessed=10**6),
    )(held[2], held[3])
    keep, send, fine = call(
        scores_kernel,
        [shaped((ROWS, HALF), F32)] * 2 + [shaped((2, HALF, WIDE), BF16)],
        [
            V((2 * OWN_IMAGES, WIDE), BF16), V((CLS_PEERS * PITCH, 128), F32),
            V((ROWS, WIDE), BF16), V((ROWS, HALF), F32),
        ],
        [V] * 4,
    )(far, held[0], held[1], class_all)
    pair = keep + along_shell(send, 1)
    other = along_shell(pair, 2)
    scores, stats = call(
        stats_kernel, [shaped((ROWS, HALF), F32), shaped((8, HALF), F32)], [], [V, V]
    )(pair, other)
    all_stats = [stats] + [along_peers(stats, k) for k in (1, 2, 3)]
    probs, evidence = call(
        probs_kernel, [shaped((ROWS, HALF), BF16), shaped((8, HALF), F32)], [], [V] * 5
    )(scores, *all_stats)
    probs_other = along_shell(probs, 1)
    evidence_other = along_shell(evidence, 1)
    own_sums = call(own_sums_kernel, shaped((CLS, WIDE), F32), [], [V, V])(probs, fine)
    sums = call(
        all_sums_kernel,
        shaped((CLS_PEERS * CHUNK, 128), BF16),
        [V((CLS, WIDE), F32), V((CLS_PEERS * PITCH, 128), F32)],
        [V] * 3,
    )(probs_other, fine, own_sums)
    own = over_classes(sums)
    new_references = call(
        final_kernel,
        shaped((CYC, OWN_CLASSES, ROW), BF16),
        [V((8 * SLOT, 128), F32), V((3, OWN_CLASSES * STEP_ROWS, 128), F32)],
        [V, V, V],
    )(offsets, own, prior_precision.reshape(1, CYC))
    mine = jnp.where(core == level // 2, evidence[0], evidence_other[0])
    log_evidence = lax.dynamic_slice_in_dim(mine, (level % 2) * OWN_IMAGES, OWN_IMAGES)
    return jnp.transpose(new_references, (1, 0, 2)), log_evidence


def solution(mesh):
    placed = (
        P("img", "shell", None),
        P("img", "shell", None),
        P(),
        P("img"),
        P(None, "shell"),
        P("shell"),
        P("shell"),
    )
    return jax.shard_map(
        local,
        mesh=mesh,
        in_specs=placed,
        out_specs=(P("img", "shell", None), P("img")),
        check_vma=False,
    )
```

```python
import functools

import jax
import jax.numpy as jnp
from jax import lax
from jax.experimental import pallas as pl
from jax.experimental.pallas import tpu as pltpu
from jax.sharding import PartitionSpec as P

ANG = 192
ROT = 48
STEP = ANG // ROT
CYC = 10
ROW = 2 * ANG
TURN = 32
TURNS = ANG // TURN
FINE = TURN // STEP
BLOCK = 2 * CYC * TURN
COEF = TURNS * BLOCK
WIDE = COEF + 128
OWN_IMAGES = 16
OWN_CLASSES = 3
IMG_PEERS = 4
CLS_PEERS = 16
CLS = OWN_CLASSES * CLS_PEERS
TILES = WIDE // 128
SLOT = 32
CHUNK = OWN_CLASSES * SLOT
PITCH = CHUNK + 8
ROWS = TURNS * CLS
HALF = FINE * OWN_IMAGES * 2
F32 = jnp.float32
BF16 = jnp.bfloat16
VMEM_LIMIT = 24 * 1024 * 1024
VMEM_MOST = 60 * 1024 * 1024


def lanes_of(shape):
    return lax.broadcasted_iota(jnp.int32, shape, len(shape) - 1)


def three_parts(x):
    hi = x.astype(BF16).astype(F32)
    rest = x - hi
    mid = rest.astype(BF16).astype(F32)
    return hi, mid, rest - mid


def pick4(lane, parts):
    return jnp.where(
        lane < 64,
        jnp.where(lane < 32, parts[0], parts[1]),
        jnp.where(lane < 96, parts[2], parts[3]),
    )


def turned_tile(rows_of, w, j, lane):
    parts = []
    for t in range(4):
        p, q = 2 * j + t // 2, t % 2
        start = q * ANG + TURN * w
        vreg, off = start // 128, start % 128
        piece = rows_of[p][:, vreg * 128 : vreg * 128 + 128]
        shift = (32 * t - off) % 128
        parts.append(pltpu.roll(piece, shift, 1) if shift else piece)
    return pick4(lane, parts)


def interleaving(back=False):
    a = lax.broadcasted_iota(jnp.int32, (128, 128), 0)
    b = lax.broadcasted_iota(jnp.int32, (128, 128), 1)
    if back:
        a, b = b, a
    return jnp.where(b == (a % TURN) * 4 + a // TURN, 1.0, 0.0).astype(BF16)


def doubled_roll(x, shift):
    lane = lanes_of(x.shape)
    other = pltpu.roll(x, ANG, 1)
    first = lane < ANG
    a0 = pltpu.roll(jnp.where(first, x, other), shift, 1)
    a1 = pltpu.roll(jnp.where(first, other, x), shift, 1)
    return jnp.where(first, a0, a1)


LANES = [slice(v * 128, v * 128 + 128) for v in range(ROW // 128)]
STEP_ROWS = 24


def turn_classes(grouped, shifts):
    for c, shift in enumerate(shifts):
        rows = slice(c * STEP_ROWS, c * STEP_ROWS + 16)
        wide = jnp.concatenate([grouped[v, rows, :] for v in range(3)], axis=1)
        wide = doubled_roll(wide, shift)
        for v, at in enumerate(LANES):
            grouped[v, rows, :] = wide[:, at]


def prologue_kernel(
    offset_ref, group_ref, images_ref, refs_ref, ctf_ref, noise_ref,
    image_msg, class_msg,
    table_f, table_s, filt, square, grouped, own,
):
    grouped[...] = jnp.zeros_like(grouped)
    for p in range(CYC):
        row = refs_ref[p].astype(F32)
        for v, at in enumerate(LANES):
            grouped[v, pl.ds(p, OWN_CLASSES, stride=STEP_ROWS), :] = row[:, at]
    turn_classes(grouped, [offset_ref[lax.axis_index("img") * OWN_CLASSES + c] for c in range(OWN_CLASSES)])
    rows = []
    for p in range(CYC):
        parts = [grouped[v, pl.ds(p, 8, stride=STEP_ROWS), :] for v in range(3)]
        rows.append(jnp.concatenate(parts, axis=1))
    lane8 = lanes_of((8, 128))
    power = jnp.zeros((8, 128), F32)
    for p in range(CYC):
        power = jnp.where(lane8 == p, jnp.sum(rows[p] * rows[p], axis=1, keepdims=True), power)
    mixing = interleaving()
    own[...] = jnp.zeros_like(own)
    for w in range(TURNS):
        tiles = [turned_tile(rows, w, j, lane8) for j in range(5)]
        tiles = jnp.concatenate(tiles, axis=0).astype(BF16)
        tiles = jnp.dot(tiles, mixing, preferred_element_type=F32)
        for j in range(5):
            own[pl.ds(w * 5 + j, OWN_CLASSES, stride=SLOT), :] = tiles[
                j * 8 : j * 8 + OWN_CLASSES
            ]
    hi, mid, lo = three_parts(-0.5 * power)
    extra = hi
    for k, part in enumerate((hi, mid, hi, mid, lo)):
        extra = extra + pltpu.roll(part, 10 * (k + 1), 1)
    own[pl.ds(TILES - 1, OWN_CLASSES, stride=SLOT), :] = extra[:OWN_CLASSES]
    held = own[...].astype(BF16)
    for d in range(CLS_PEERS):
        class_msg[d * CHUNK : (d + 1) * CHUNK, :] = held

    weight = 1.0 / noise_ref[...]
    ctf = ctf_ref[...]
    table_f[...] = jnp.zeros_like(table_f)
    table_s[...] = jnp.zeros_like(table_s)
    table_f[:, :CYC] = ctf * weight
    table_s[:, :CYC] = ctf * ctf * weight
    for i in range(OWN_IMAGES):
        g = group_ref[i]
        filt[i : i + 1, :] = table_f[pl.ds(g, 1), :]
        square[i : i + 1, :] = table_s[pl.ds(g, 1), :]
    lane16 = lanes_of((OWN_IMAGES, 128))
    factors = filt[...]
    rows = []
    for p in range(CYC):
        x = images_ref[p] * factors[:, p : p + 1]
        rows.append(x.astype(BF16).astype(F32))
    for w in range(TURNS):
        tiles = [turned_tile(rows, w, j, lane16) for j in range(5)]
        tiles = jnp.concatenate(tiles, axis=0).astype(BF16)
        tiles = jnp.dot(tiles, mixing, preferred_element_type=F32).astype(BF16)
        for j in range(5):
            at = w * BLOCK + j * 128
            image_msg[:, at : at + 128] = tiles[j * 16 : j * 16 + 16]
    hi, mid, lo = three_parts(square[...])
    extra = hi
    for k, part in enumerate((mid, hi, lo, mid, hi)):
        extra = extra + pltpu.roll(part, 10 * (k + 1), 1)
    image_msg[:, COEF:] = extra.astype(BF16)


def turned_on(cur, nxt, steps):
    s = 4 * STEP * steps
    lane = lanes_of(cur.shape)
    return pltpu.roll(jnp.where(lane >= s, cur, nxt), 128 - s, 1)


def tile_pairs():
    for w in range(TURNS):
        for j in range(5):
            here = w * BLOCK + j * 128
            there = (w + 1) % TURNS * BLOCK + j * 128
            yield slice(here, here + 128), slice(there, there + 128)


def fill_fine(images_ref, fine_ref):
    for rho in range(FINE):
        fine_ref[32 * rho : 32 * rho + 32, COEF:] = images_ref[:, COEF:]
    for here, there in tile_pairs():
        cur, nxt = images_ref[:, here], images_ref[:, there]
        fine_ref[:32, here] = cur
        for rho in range(1, FINE):
            fine_ref[32 * rho : 32 * rho + 32, here] = turned_on(cur, nxt, rho)


def place():
    return lax.axis_index("img") // IMG_PEERS % IMG_PEERS, lax.axis_index("shell") % 2


def gather_pair(pair, to_ref):
    level, _ = place()
    for k, ref in enumerate(pair):
        at = pl.multiple_of(((level & 1) ^ k) * OWN_IMAGES, 16)
        to_ref[pl.ds(at, OWN_IMAGES), :] = ref[...]


def early_kernel(f2, f3, fine_ref, pair):
    gather_pair((f2, f3), pair)
    fill_fine(pair, fine_ref)


def is_near():
    level, core = place()
    return (level >> 1) == core


NT = (((1,), (1,)), ((), ()))


def scores_kernel(
    far_ref, f0, f1, class_ref, keep_ref, send_ref, fine_ref, pair, wide, stack, part
):
    gather_pair((f0, f1), pair)
    for d in range(CLS_PEERS):
        wide[d * PITCH : d * PITCH + CHUNK, :] = class_ref[d * CHUNK : (d + 1) * CHUNK, :].astype(F32)
    for v in range(TILES):
        for c in range(OWN_CLASSES):
            tile = wide[pl.ds(c * SLOT + v, CLS_PEERS, stride=PITCH), :].astype(BF16)
            for g in range(TURNS):
                row = g * CLS + c * CLS_PEERS
                at = v * 128 if v == TILES - 1 else (v * 128 + g * BLOCK) % COEF
                stack[row : row + CLS_PEERS, at : at + 128] = tile
    part[...] = lax.dot_general(stack[...], far_ref[...], NT, preferred_element_type=F32)
    fill_fine(pair, fine_ref.at[0])
    fine_ref[1] = far_ref[...]
    last = lax.dot_general(stack[...], fine_ref[0], NT, preferred_element_type=F32)
    first = part[...]
    near = is_near()
    keep_ref[...] = jnp.where(near, last, first)
    send_ref[...] = jnp.where(near, first, last)


def over_rotations(op, x):
    for s in (32, 64, 128):
        x = op(x, pltpu.roll(x, s, 1))
    return x


def stats_kernel(mine_ref, other_ref, scores_ref, stats_ref):
    scores = mine_ref[...] + other_ref[...]
    scores_ref[...] = scores
    big = jnp.max(scores, axis=0, keepdims=True)
    big = over_rotations(jnp.maximum, jnp.broadcast_to(big, (8, HALF)))
    part = jnp.sum(jnp.exp(scores - big[:1]), axis=0, keepdims=True)
    part = over_rotations(jnp.add, jnp.broadcast_to(part, (8, HALF)))
    row = lax.broadcasted_iota(jnp.int32, (8, HALF), 0)
    stats_ref[...] = jnp.where(row < 4, big, part)


def probs_kernel(scores_ref, s0, s1, s2, s3, probs_ref, evidence_ref):
    stats = [s[...] for s in (s0, s1, s2, s3)]
    bigs = [s[0:1] for s in stats]
    parts = [s[4:5] for s in stats]
    largest = jnp.maximum(jnp.maximum(bigs[0], bigs[1]), jnp.maximum(bigs[2], bigs[3]))
    total = sum(p * jnp.exp(b - largest) for b, p in zip(bigs, parts))
    evidence = largest + jnp.log(total)
    probs_ref[...] = jnp.exp(scores_ref[...] - evidence).astype(BF16)
    evidence_ref[...] = jnp.broadcast_to(evidence, (8, HALF))


def add_turns(probs_ref, fine_ref, sums, base):
    for w in range(0, TURNS, 2):
        span = slice(w * BLOCK, (w + 2) * BLOCK + (128 if w == TURNS - 2 else 0))
        turned = jnp.dot(probs_ref[...], fine_ref[:, span], preferred_element_type=F32)
        for b in (w, w + 1):
            for g in range(TURNS):
                back = (b - g) % TURNS
                at = slice(back * BLOCK, (back + 1) * BLOCK)
                term = turned[g * CLS : (g + 1) * CLS, (b - w) * BLOCK : (b - w + 1) * BLOCK]
                if b == 0:
                    sums[:, at] = term if base is None else base[:, at] + term
                else:
                    sums[:, at] += term
        if w == TURNS - 2:
            mass = turned[:CLS, 2 * BLOCK :]
            for g in range(1, TURNS):
                mass = mass + turned[g * CLS : (g + 1) * CLS, 2 * BLOCK :]
    return mass


def own_sums_kernel(probs_ref, fine_ref, sums_ref):
    mine = fine_ref.at[jnp.where(is_near(), 0, 1)]
    sums_ref[:, COEF:] = add_turns(probs_ref, mine, sums_ref, None)


def all_sums_kernel(probs_ref, fine_ref, own_ref, out_ref, sums, packed):
    rest = fine_ref.at[jnp.where(is_near(), 1, 0)]
    mass = own_ref[:, COEF:] + add_turns(probs_ref, rest, sums, own_ref)
    mass = mass + pltpu.roll(mass, 118, 1) + pltpu.roll(mass, 98, 1)
    mass = jnp.where(lanes_of((CLS, 128)) < CYC, mass, 0.0)
    hi, mid, lo = three_parts(mass)
    sums[:, COEF:] = hi + pltpu.roll(mid, 10, 1) + pltpu.roll(lo, 20, 1)
    for c in range(OWN_CLASSES):
        rows = slice(c * CLS_PEERS, (c + 1) * CLS_PEERS)
        for v in range(SLOT):
            tile = sums[rows, v * 128 : v * 128 + 128] if v < TILES else jnp.zeros((16, 128), F32)
            packed[pl.ds(c * SLOT + v, CLS_PEERS, stride=PITCH), :] = tile
    for d in range(CLS_PEERS):
        out_ref[d * CHUNK : (d + 1) * CHUNK, :] = packed[d * PITCH : d * PITCH + CHUNK, :].astype(BF16)


def final_kernel(offset_ref, msg_ref, prior_ref, out_ref, summed, grouped):
    total = msg_ref[:CHUNK, :].astype(F32)
    for d in range(1, CLS_PEERS):
        total = total + msg_ref[d * CHUNK : (d + 1) * CHUNK, :].astype(F32)
    summed[:CHUNK, :] = total
    summed[CHUNK:, :] = jnp.zeros((8 * SLOT - CHUNK, 128), F32)
    lane = lanes_of((8, 128))
    extra = summed[pl.ds(TILES - 1, 8, stride=SLOT), :]
    den = extra + pltpu.roll(extra, 118, 1) + pltpu.roll(extra, 108, 1)
    tiles = {}
    for j in range(5):
        below = []
        for p in (2 * j, 2 * j + 1):
            below.append(den[:, p : p + 1] + prior_ref[0:1, p : p + 1])
        below = jnp.where(lane % 4 < 2, below[0], below[1])
        for w in range(TURNS):
            tiles[w, j] = summed[pl.ds(w * 5 + j, 8, stride=SLOT), :] / below
    keys = list(tiles)
    flat = jnp.concatenate([tiles[k] for k in keys], axis=0).astype(BF16)
    flat = jnp.dot(flat, interleaving(back=True), preferred_element_type=F32)
    tiles = {k: flat[8 * n : 8 * n + 8] for n, k in enumerate(keys)}
    grouped[...] = jnp.zeros_like(grouped)
    for p in range(CYC):
        for v in range(3):
            parts = []
            for u in range(4):
                start = 128 * v + 32 * u
                q, w = start // ANG, (start % ANG) // TURN
                t = 2 * (p % 2) + q
                shift = (32 * u - 32 * t) % 128
                piece = tiles[w, p // 2]
                parts.append(pltpu.roll(piece, shift, 1) if shift else piece)
            grouped[v, pl.ds(p, OWN_CLASSES, stride=STEP_ROWS), :] = pick4(lane, parts)[
                :OWN_CLASSES
            ]
    shifts = []
    for c in range(OWN_CLASSES):
        off = offset_ref[0, c]
        shifts.append(jnp.where(off == 0, 0, ROW - off))
    turn_classes(grouped, shifts)
    for p in range(CYC):
        for v, at in enumerate(LANES):
            out_ref[p, :, at] = grouped[v, pl.ds(p, OWN_CLASSES, stride=STEP_ROWS), :].astype(BF16)


def call(kernel, outs, scratch, specs, limit=VMEM_LIMIT, cost=None):
    return pl.pallas_call(
        kernel,
        out_shape=outs,
        in_specs=[pl.BlockSpec(memory_space=s) for s in specs],
        out_specs=jax.tree.map(lambda _: pl.BlockSpec(memory_space=pltpu.VMEM), outs),
        scratch_shapes=scratch,
        compiler_params=pltpu.CompilerParams(vmem_limit_bytes=limit),
        cost_estimate=cost,
    )


S, V = pltpu.SMEM, pltpu.VMEM


def shaped(shape, dtype):
    return jax.ShapeDtypeStruct(shape, dtype)


def local(images, references, class_offset, ctf_group, ctf, noise_power, prior_precision):
    img = lax.axis_index("img")
    level, core = place()
    offsets = lax.dynamic_slice_in_dim(class_offset, img * OWN_CLASSES, OWN_CLASSES).reshape(1, -1)

    def along_peers(x, k):
        return lax.ppermute(x, "img", [(i, i ^ (4 * k)) for i in range(64)])

    def along_shell(x, k):
        return lax.ppermute(x, "shell", [(i, i ^ k) for i in range(4)])

    groups = [[16 * y + 4 * z + x for y in range(4) for x in range(4)] for z in range(4)]

    def over_classes(x):
        return lax.all_to_all(x, "img", 0, 0, axis_index_groups=groups, tiled=True)

    image_msg, class_msg = call(
        prologue_kernel,
        [shaped((OWN_IMAGES, WIDE), BF16), shaped((CLS_PEERS * CHUNK, 128), BF16)],
        [V((16, 128), F32)] * 4 + [V((3, 8 * STEP_ROWS, 128), F32), V((CHUNK, 128), F32)],
        [S, S, V, V, V, V],
        VMEM_MOST,
    )(
        class_offset, ctf_group, jnp.transpose(images, (1, 0, 2)),
        jnp.transpose(references, (1, 0, 2)), ctf, noise_power.reshape(1, CYC),
    )
    held = [image_msg] + [along_peers(image_msg, k) for k in (1, 2, 3)]
    class_all = over_classes(class_msg)
    far = call(
        early_kernel,
        shaped((HALF, WIDE), BF16),
        [V((2 * OWN_IMAGES, WIDE), BF16)],
        [V, V],
        cost=pl.CostEstimate(flops=26 * 10**8, transcendentals=0, bytes_accessed=10**6),
    )(held[2], held[3])
    keep, send, fine = call(
        scores_kernel,
        [shaped((ROWS, HALF), F32)] * 2 + [shaped((2, HALF, WIDE), BF16)],
        [
            V((2 * OWN_IMAGES, WIDE), BF16), V((CLS_PEERS * PITCH, 128), F32),
            V((ROWS, WIDE), BF16), V((ROWS, HALF), F32),
        ],
        [V] * 4,
    )(far, held[0], held[1], class_all)
    pair = keep + along_shell(send, 1)
    other = along_shell(pair, 2)
    scores, stats = call(
        stats_kernel, [shaped((ROWS, HALF), F32), shaped((8, HALF), F32)], [], [V, V]
    )(pair, other)
    all_stats = [stats] + [along_peers(stats, k) for k in (1, 2, 3)]
    probs, evidence = call(
        probs_kernel, [shaped((ROWS, HALF), BF16), shaped((8, HALF), F32)], [], [V] * 5
    )(scores, *all_stats)
    probs_other = along_shell(probs, 1)
    evidence_other = along_shell(evidence, 1)
    own_sums = call(own_sums_kernel, shaped((CLS, WIDE), F32), [], [V, V])(probs, fine)
    sums = call(
        all_sums_kernel,
        shaped((CLS_PEERS * CHUNK, 128), BF16),
        [V((CLS, WIDE), F32), V((CLS_PEERS * PITCH, 128), F32)],
        [V] * 3,
    )(probs_other, fine, own_sums)
    own = over_classes(sums)
    new_references = call(
        final_kernel,
        shaped((CYC, OWN_CLASSES, ROW), BF16),
        [V((8 * SLOT, 128), F32), V((3, OWN_CLASSES * STEP_ROWS, 128), F32)],
        [V, V, V],
    )(offsets, own, prior_precision.reshape(1, CYC))
    mine = jnp.where(core == level // 2, evidence[0], evidence_other[0])
    log_evidence = lax.dynamic_slice_in_dim(mine, (level % 2) * OWN_IMAGES, OWN_IMAGES)
    return jnp.transpose(new_references, (1, 0, 2)), log_evidence


def solution(mesh):
    placed = (
        P("img", "shell", None),
        P("img", "shell", None),
        P(),
        P("img"),
        P(None, "shell"),
        P("shell"),
        P("shell"),
    )
    return jax.shard_map(
        local,
        mesh=mesh,
        in_specs=placed,
        out_specs=(P("img", "shell", None), P("img")),
        check_vma=False,
    )
```
